256 devices in a mesh: dp: 16 (over y_lo, x, core), tensor: 16 (over y_hi, z).
Axes of the slice: x: 4, y: 4 (y_hi: 2, y_lo: 2; y = y_hi * 2 + y_lo), z: 8, core: 2. Of those that a mesh axis runs over, the one named last changes fastest.
Arguments:
- hidden: bfloat16 [4096, 18432], P('dp', 'tensor'), may hold values from -0.75 to 0.75
- out_grad: bfloat16 [4096, 2304], P('dp'), may hold values from -1 to 1
- weight: bfloat16 [18432, 2304], P('tensor'), may hold values from -0.046875 to 0.046875
- first_moment: float32 [2304, 18432], P('dp', 'tensor'), may hold values from -3 to 3
- second_moment: float32 [2304, 18432], P('dp', 'tensor'), may hold values from 0.1 to 4
- next_hidden: bfloat16 [4096, 18432], P('dp', 'tensor'), may hold values from -6 to 6
Outputs:
- input_grad: bfloat16 [4096, 18432], P('dp', 'tensor')
- first_new: float32 [2304, 18432], P('dp', 'tensor')
- second_new: float32 [2304, 18432], P('dp', 'tensor')
- new_weight: bfloat16 [2304, 18432], P('dp', 'tensor')
- next_out: bfloat16 [4096, 2304], P('dp')
The draws below stay inside these ranges and needn't reach their ends.
All inputs are finite; a program needn't handle non-finite values.
Results may differ from the reference program's by a relative error of at most 0.007.
Values may be sent and summed in bfloat16 or wider, within the bound.
No kernel may reach another device: no remote copies, remote signals or barrier semaphores. Data moves between devices by JAX's collectives and lax.ppermute only.
A program may use at most 128 MiB of HBM per device.

```python
import math
import jax
import jax.numpy as jnp

D = 2304
FF = 18432
TOKENS = 4096


def strengthened(entries, rng, source, target, parts, factor):
    owner, partner = [(jnp.arange(entries.shape[position]) // (entries.shape[position] // parts)).reshape([-1 if axis == position else 1 for axis in range(entries.ndim)]) for position in (source, target)]
    chosen = jax.random.permutation(rng, parts)[partner]
    strong = (owner == chosen) | (owner == (partner + parts // 2) % parts)
    return jnp.where(strong, factor * entries, entries)


def levels(key, dims, pieces, least, high):
    level = 1.0
    for position, parts in pieces:
        steps = jax.random.uniform(jax.random.fold_in(jax.random.fold_in(key, 6), position), (parts,), jnp.float32, least / len(pieces), high / len(pieces))
        level = level * jnp.repeat(jnp.exp(steps), dims[position] // parts).reshape((-1,) + (1,) * (len(dims) - 1 - position))
    return level


def normal_values(key, shape, scale, most, shards=(), dtype=jnp.bfloat16):
    result = scale * jax.random.normal(key, shape, jnp.float32)
    if shards:
        result = result * levels(key, shape, shards, -0.22, 0.18)
    return jnp.clip(result, -most, most).astype(dtype)


def gaussian_with(stream_key, extent, width, limit, split, heavy, held_as=jnp.bfloat16):
    drawn = width * jax.random.normal(stream_key, extent, jnp.float32)
    if split:
        drawn = drawn * levels(stream_key, extent, split, -0.22, 0.18)
    return jnp.clip(strengthened(drawn, jax.random.fold_in(stream_key, 3), *heavy), -limit, limit).astype(held_as)


def setup_inputs(seed: int = 0) -> dict:
    keys = jax.random.split(jax.random.key(seed), 7)
    return {
        "hidden": normal_values(keys[0], (TOKENS, FF), (TOKENS ** -0.25), 0.75, ((0, 16), (1, 16))),
        "out_grad": gaussian_with(keys[1], (TOKENS, D), (TOKENS ** -0.25), 1.0, ((0, 16),), (0, 1, 16, 2.0)),
        "weight": normal_values(keys[2], (FF, D), FF ** -0.5, 0.046875, ((0, 16),)),
        "first_moment": normal_values(keys[3], (D, FF), 0.5, 3.0, ((0, 16), (1, 16)), jnp.float32),
        "second_moment": jnp.clip(jnp.exp(math.log(4.0) - 3.6888794 * jax.random.uniform(keys[4], (D, FF), jnp.float32) ** levels(keys[4], (D, FF), ((0, 16), (1, 16)), -0.2, 0.2)), 0.1, 4.0),
        "next_hidden": normal_values(keys[5], (TOKENS, FF), 1.0, 6.0, ((0, 16), (1, 16))),
    }


beta_first = 0.9
beta_second = 0.95
learn_rate = 0.001
weight_decay = 0.1
epsilon = 1e-08
correct_first = 0.999973438601112
correct_second = 0.99407947077967

def reference(hidden, out_grad, weight, first_moment, second_moment, next_hidden):
    input_grad = jnp.dot(out_grad, weight.T, preferred_element_type=jnp.float32).astype(jnp.bfloat16)
    grad = jnp.dot(out_grad.T, hidden, preferred_element_type=jnp.float32)
    first_new = beta_first * first_moment + (1.0 - beta_first) * grad
    second_new = beta_second * second_moment + (1.0 - beta_second) * grad * grad
    current = weight.T.astype(jnp.float32)
    update = first_new / correct_first / (jnp.sqrt(second_new / correct_second) + epsilon)
    new_weight = (current - learn_rate * (update + weight_decay * current)).astype(jnp.bfloat16)
    next_out = jnp.dot(next_hidden, new_weight.T, preferred_element_type=jnp.float32).astype(jnp.bfloat16)
    return (input_grad, first_new, second_new, new_weight, next_out)
```

```python
import functools

import jax
import jax.numpy as jnp
import numpy as np
from jax import lax
from jax.experimental import pallas as pl
from jax.experimental.pallas import tpu as pltpu
from jax.sharding import PartitionSpec as P

beta_first = 0.9
beta_second = 0.95
learn_rate = 0.001
weight_decay = 0.1
epsilon = 1e-08
correct_first = 0.999973438601112
correct_second = 0.99407947077967

BF = jnp.bfloat16
F32 = jnp.float32
MB = 1024 * 1024

GRAY = (0, 1, 3, 2)
CORE, X1, X2, Y = 1, 2, 4, 8
ENC = [(d % 2) | (GRAY[(d // 2) % 4] << 1) | ((d // 8) << 3) for d in range(16)]
DEC = [ENC.index(r) for r in range(16)]
ORDERS = ((X1, X2, Y), (X2, Y, X1), (Y, X1, X2))
PARTS = len(ORDERS)


def flip(mask):
    return [(d, DEC[ENC[d] ^ mask]) for d in range(16)]


def relative(order, q):
    return (
        (q >> 3 & 1) * CORE
        | (q >> 2 & 1) * order[0]
        | (q >> 1 & 1) * order[1]
        | (q & 1) * order[2]
    )


PLACE = np.array(
    [
        [[DEC[ENC[d] ^ relative(order, q)] for q in range(16)] for order in ORDERS]
        for d in range(16)
    ],
    np.int32,
)


def swap(value, mask):
    return lax.ppermute(value, "dp", flip(mask))


def grad_half(first, block, table, source, hidden, *rest):
    if first:
        out, turned, lhs = rest
        turned[...] = source[...].T
    else:
        out, lhs = rest
        turned = source
    start = 8 if first else 0
    width = hidden.shape[1] // PARTS
    for part in range(PARTS):
        for q in range(8):
            row = pl.multiple_of(table[part * 16 + start + q] * block, block)
            lhs[q * block : (q + 1) * block, :] = turned[pl.ds(row, block), :]
        out[part] = jnp.dot(
            lhs[...], hidden[:, part * width : (part + 1) * width], preferred_element_type=F32
        ).astype(BF)


def vmem():
    return pl.BlockSpec(memory_space=pltpu.VMEM)


def smem():
    return pl.BlockSpec(memory_space=pltpu.SMEM)


def call_grad(first, table, source, hidden):
    tokens = hidden.shape[0]
    features = source.shape[1] if first else source.shape[0]
    block = features // 16
    half = jax.ShapeDtypeStruct((PARTS, features // 2, hidden.shape[1] // PARTS), BF)
    flops = tokens * features * hidden.shape[1]
    return pl.pallas_call(
        functools.partial(grad_half, first, block),
        out_shape=(half, jax.ShapeDtypeStruct((features, tokens), BF)) if first else half,
        in_specs=[smem(), vmem(), vmem()],
        out_specs=(vmem(), vmem()) if first else vmem(),
        scratch_shapes=[pltpu.VMEM((features // 2, tokens), BF)],
        compiler_params=pltpu.CompilerParams(vmem_limit_bytes=40 * MB),
        cost_estimate=pl.CostEstimate(flops=flops, bytes_accessed=6 * MB, transcendentals=0),
    )(table, source, hidden)


def next_product(block, table, hidden, s0, s1, s2, s3, c1, c2, c3, out, full):
    width = hidden.shape[1] // PARTS
    for part in range(PARTS):
        columns = slice(part * width, (part + 1) * width)
        q = 0
        for ref in (s0, s1, s2, s3, c1, c2, c3):
            for k in range(ref.shape[1] // block):
                row = pl.multiple_of(table[part * 16 + q] * block, block)
                full[pl.ds(row, block), columns] = ref[part, k * block : (k + 1) * block, :]
                q += 1
    out[...] = lax.dot_general(
        hidden[...], full[...], (((1,), (1,)), ((), ())), preferred_element_type=F32
    ).astype(BF)


def call_product(table, hidden, pieces, features):
    tokens, units = hidden.shape
    return pl.pallas_call(
        functools.partial(next_product, features // 16),
        out_shape=jax.ShapeDtypeStruct((tokens, features), BF),
        in_specs=[smem()] + [vmem()] * 8,
        out_specs=vmem(),
        scratch_shapes=[pltpu.VMEM((features, units), BF)],
        compiler_params=pltpu.CompilerParams(vmem_limit_bytes=40 * MB),
        cost_estimate=pl.CostEstimate(
            flops=2 * tokens * units * features, bytes_accessed=8 * MB, transcendentals=0
        ),
    )(table, hidden, *pieces)


def total(terms):
    result = terms[0].astype(F32)
    for term in terms[1:]:
        result = result + term.astype(F32)
    return result


def shards(hidden, out_grad, weight, first_moment, second_moment, next_hidden):
    columns = first_moment.shape[0]
    features = out_grad.shape[1]
    device = lax.axis_index("dp")
    table = lax.dynamic_index_in_dim(
        jnp.asarray(PLACE.reshape(16, -1)), device, 0, keepdims=False
    )

    sent, turned = call_grad(True, table, out_grad, hidden)
    crossed = swap(sent, CORE)
    kept = call_grad(False, table, turned, hidden)
    input_grad = lax.dot_general(
        out_grad, weight, (((1,), (1,)), ((), ())), preferred_element_type=F32
    ).astype(BF)
    sums = [[kept[p], crossed[p]] for p in range(PARTS)]
    for step in range(3):
        rows = features >> (step + 2)
        for p in range(PARTS):
            mine = total([term[rows : 2 * rows] for term in sums[p]]).astype(BF)
            sums[p] = [term[:rows] for term in sums[p]] + [swap(mine, ORDERS[p][step])]
    grad = jnp.concatenate([total(terms) for terms in sums], axis=1)

    first_new = beta_first * first_moment + (1.0 - beta_first) * grad
    second_new = beta_second * second_moment + (1.0 - beta_second) * grad * grad
    current = lax.dynamic_slice_in_dim(weight, device * columns, columns, 1).astype(F32).T
    update = first_new / correct_first / (jnp.sqrt(second_new / correct_second) + epsilon)
    new_weight = (current - learn_rate * (update + weight_decay * current)).astype(BF)

    own = jnp.stack(jnp.split(new_weight, PARTS, axis=1))
    held = [own[p] for p in range(PARTS)]
    arrived = []
    for step in (2, 1, 0):
        got = [swap(held[p], ORDERS[p][step]) for p in range(PARTS)]
        arrived.append(jnp.stack(got))
        if step:
            held = [jnp.concatenate([held[p], got[p]]) for p in range(PARTS)]
    passed = [
        swap(jnp.concatenate([own, arrived[0]], axis=1), CORE),
        swap(arrived[1], CORE),
        swap(arrived[2], CORE),
    ]
    part_out = call_product(table, next_hidden, [own] + arrived + passed, features)

    shares = lax.all_to_all(part_out, "tensor", 0, 0, tiled=True)
    share = total(list(jnp.split(shares, 16))).astype(BF)
    next_out = lax.all_to_all(
        jnp.concatenate([share] * 16), "tensor", 0, 0, tiled=True
    )
    return (input_grad, first_new, second_new, new_weight, next_out)


def solution(mesh):
    placed = (
        P("dp", "tensor"),
        P("dp", None),
        P("tensor", None),
        P("dp", "tensor"),
        P("dp", "tensor"),
        P("dp", "tensor"),
    )
    return jax.shard_map(
        shards,
        mesh=mesh,
        in_specs=placed,
        out_specs=(
            P("dp", "tensor"),
            P("dp", "tensor"),
            P("dp", "tensor"),
            P("dp", "tensor"),
            P("dp", None),
        ),
        check_vma=False,
    )
```

```python
import functools

import jax
import jax.numpy as jnp
import numpy as np
from jax import lax
from jax.experimental import pallas as pl
from jax.experimental.pallas import tpu as pltpu
from jax.sharding import PartitionSpec as P

beta_first = 0.9
beta_second = 0.95
learn_rate = 0.001
weight_decay = 0.1
epsilon = 1e-08
correct_first = 0.999973438601112
correct_second = 0.99407947077967

BF = jnp.bfloat16
F32 = jnp.float32
MB = 1024 * 1024

GRAY = (0, 1, 3, 2)
CORE, X1, X2, Y = 1, 2, 4, 8
ENC = [(d % 2) | (GRAY[(d // 2) % 4] << 1) | ((d // 8) << 3) for d in range(16)]
DEC = [ENC.index(r) for r in range(16)]
ORDERS = (((X1, Y, X2), (X2, X1, Y)), ((Y, X2, X1), (Y, X2, X1)))
PARTS = 2


def flip(masks):
    return [(d, DEC[ENC[d] ^ masks[d % 2]]) for d in range(16)]


def relative(order, q):
    return (q >> 2 & 1) * order[0] | (q >> 1 & 1) * order[1] | (q & 1) * order[2]


PLACE = np.array(
    [
        [[DEC[ENC[d] ^ relative(ORDERS[p][d % 2], q)] // 2 for q in range(8)] for p in range(PARTS)]
        for d in range(16)
    ],
    np.int32,
)


def swap(value, part, step):
    return lax.ppermute(value, "dp", flip([order[step] for order in ORDERS[part]]))


def swap_cores(value):
    return lax.ppermute(value, "dp", flip((CORE, CORE)))


def aligned(index, size):
    return pl.ds(pl.multiple_of(index * size, size), size)


def place(table, device, part, q):
    return table[(device * PARTS + part) * 8 + q]


def turn(block, device, out_grad, own, other, turned):
    turned[...] = out_grad[...].T
    parity = device[0] % 2
    for i in range(8):
        rows = slice(i * block, (i + 1) * block)
        own[rows, :] = turned[aligned(2 * i + parity, block), :]
        other[rows, :] = turned[aligned(2 * i + 1 - parity, block), :]


def grad_half(start, cuts, block, device, table, own, got, hidden, hidden_got, *rest):
    outs, lhs, rhs = rest[:PARTS], rest[PARTS], rest[PARTS + 1]
    tokens = hidden.shape[0]
    rhs[:tokens, :] = hidden[...]
    rhs[tokens:, :] = hidden_got[...]
    for part in range(PARTS):
        for q in range(4):
            rows = slice(q * block, (q + 1) * block)
            from_rows = aligned(place(table, device[0], part, start + q), block)
            lhs[part, rows, :tokens] = own[from_rows, :]
            lhs[part, rows, tokens:] = got[from_rows, :]
        outs[part][...] = jnp.dot(
            lhs[part], rhs[:, cuts[part] : cuts[part + 1]], preferred_element_type=F32
        ).astype(BF)


def product_rows(half, hidden, hidden_got, lhs, upper):
    wanted = 1 - upper if half else upper
    share = 16
    for z in range(8):
        rows = aligned(wanted * 8 + z, share)
        lhs[2 * z * share : (2 * z + 1) * share, :] = hidden[rows, :]
        lhs[(2 * z + 1) * share : (2 * z + 2) * share, :] = hidden_got[rows, :]


def contract(lhs, full):
    return lax.dot_general(
        lhs[...], full[...], (((1,), (1,)), ((), ())), preferred_element_type=F32
    ).astype(BF)


def product_sent(cuts, block, device, upper, table, hidden, hidden_got, *rest):
    pieces, (out, full, lhs) = rest[:-3], rest[-3:]
    per_part = len(pieces) // PARTS
    for part in range(PARTS):
        columns = slice(cuts[part], cuts[part + 1])
        q = 0
        for ref in pieces[part * per_part : (part + 1) * per_part]:
            for k in range(ref.shape[0] // block):
                to_rows = aligned(place(table, device[0], part, q), block)
                full[to_rows, columns] = ref[k * block : (k + 1) * block, :]
                q += 1
    product_rows(True, hidden, hidden_got, lhs, upper[0])
    out[...] = contract(lhs, full)


def product_kept(upper, hidden, hidden_got, full, out, lhs):
    product_rows(False, hidden, hidden_got, lhs, upper[0])
    out[...] = contract(lhs, full)


def spread(block, device, own, got, out):
    parity = device[0] % 2
    mine, theirs = own[...].astype(F32), got[...].astype(F32)
    even = jnp.where(parity == 0, mine, theirs)
    odd = jnp.where(parity == 0, theirs, mine)
    pieces = []
    for i in range(8):
        columns = slice(i * block, (i + 1) * block)
        pieces += [even[:, columns], odd[:, columns]]
    value = jnp.concatenate(pieces, axis=1).astype(BF)
    for t in range(out.shape[0]):
        out[t] = value


def shape(*dims):
    return jax.ShapeDtypeStruct(dims, BF)


def call(kernel, out_shape, scalars, arrays, scratch, flops=0):
    vmem = pl.BlockSpec(memory_space=pltpu.VMEM)
    smem = pl.BlockSpec(memory_space=pltpu.SMEM)
    return pl.pallas_call(
        kernel,
        out_shape=out_shape,
        in_specs=[smem] * len(scalars) + [vmem] * len(arrays),
        out_specs=jax.tree.map(lambda _: vmem, out_shape),
        scratch_shapes=[pltpu.VMEM(dims, BF) for dims in scratch],
        compiler_params=pltpu.CompilerParams(vmem_limit_bytes=40 * MB),
        cost_estimate=pl.CostEstimate(
            flops=flops, bytes_accessed=sum(a.size * 2 for a in arrays), transcendentals=0
        ),
    )(*scalars, *arrays)


def total(terms):
    result = terms[0].astype(F32)
    for term in terms[1:]:
        result = result + term.astype(F32)
    return result


def shards(hidden, out_grad, weight, first_moment, second_moment, next_hidden):
    block = first_moment.shape[0]
    tokens, units = hidden.shape
    features = out_grad.shape[1]
    cuts = (0, units // 3 * 2, units)
    position = lax.axis_index("dp")
    device = position.reshape(1)
    upper = (lax.axis_index("tensor") // 8).reshape(1)
    table = jnp.asarray(PLACE.reshape(-1))

    hidden_got = swap_cores(hidden)
    own, other = call(
        functools.partial(turn, block),
        (shape(features // 2, tokens), shape(features // 2, tokens)),
        [device],
        [out_grad],
        [(features, tokens)],
    )
    got = swap_cores(other)
    halves = []
    for start in (4, 0):
        halves.append(
            call(
                functools.partial(grad_half, start, cuts, block),
                tuple(shape(4 * block, cuts[p + 1] - cuts[p]) for p in range(PARTS)),
                [device, table],
                [own, got, hidden, hidden_got],
                [(PARTS, 4 * block, 2 * tokens), (2 * tokens, units)],
                flops=2 * tokens * units * features // 2,
            )
        )
    sent, kept = halves
    sums = [[kept[p], swap(sent[p], p, 0)] for p in range(PARTS)]
    next_got = swap_cores(next_hidden)
    input_grad = lax.dot_general(
        out_grad, weight, (((1,), (1,)), ((), ())), preferred_element_type=F32
    ).astype(BF)
    for step in (1, 2):
        rows = 4 * block >> step
        for p in range(PARTS):
            mine = total([term[rows : 2 * rows] for term in sums[p]]).astype(BF)
            sums[p] = [term[:rows] for term in sums[p]] + [swap(mine, p, step)]
    grad = jnp.concatenate([total(terms) for terms in sums], axis=1)

    first_new = beta_first * first_moment + (1.0 - beta_first) * grad
    second_new = beta_second * second_moment + (1.0 - beta_second) * grad * grad
    current = lax.dynamic_slice_in_dim(weight, position * block, block, 1).astype(F32).T
    update = first_new / correct_first / (jnp.sqrt(second_new / correct_second) + epsilon)
    new_weight = (current - learn_rate * (update + weight_decay * current)).astype(BF)

    pieces = []
    for p in range(PARTS):
        pieces.append([new_weight[:, cuts[p] : cuts[p + 1]]])
    for step in (2, 1, 0):
        for p in range(PARTS):
            pieces[p].append(swap(jnp.concatenate(pieces[p]), p, step))
    sent_out, full = call(
        functools.partial(product_sent, cuts, block),
        (shape(tokens, features // 2), shape(features // 2, units)),
        [device, upper, table],
        [next_hidden, next_got] + pieces[0] + pieces[1],
        [(tokens, units)],
        flops=tokens * units * features,
    )

    across = lax.ppermute(sent_out, "tensor", [(t, (t + 8) % 16) for t in range(16)])
    kept_out = call(
        product_kept,
        shape(tokens, features // 2),
        [upper],
        [next_hidden, next_got, full],
        [(tokens, units)],
        flops=tokens * units * features,
    )
    shares = lax.all_to_all(
        total([kept_out, across]).astype(BF),
        "tensor",
        0,
        0,
        axis_index_groups=[list(range(8)), list(range(8, 16))],
        tiled=True,
    )
    share = jnp.sum(shares.reshape(8, 2, 16, -1).astype(F32), axis=0).astype(BF)
    lacking = swap_cores(share[1])
    copies = call(
        functools.partial(spread, block),
        shape(16, 16, features),
        [device],
        [share[0], lacking],
        [],
    )
    next_out = lax.all_to_all(copies, "tensor", 0, 0).reshape(tokens, features)
    return (input_grad, first_new, second_new, new_weight, next_out)


def solution(mesh):
    placed = (
        P("dp", "tensor"),
        P("dp", None),
        P("tensor", None),
        P("dp", "tensor"),
        P("dp", "tensor"),
        P("dp", "tensor"),
    )
    return jax.shard_map(
        shards,
        mesh=mesh,
        in_specs=placed,
        out_specs=(
            P("dp", "tensor"),
            P("dp", "tensor"),
            P("dp", "tensor"),
            P("dp", "tensor"),
            P("dp", None),
        ),
        check_vma=False,
    )
```

```python
import functools

import jax
import jax.numpy as jnp
import numpy as np
from jax import lax
from jax.experimental import pallas as pl
from jax.experimental.pallas import tpu as pltpu
from jax.sharding import PartitionSpec as P

beta_first = 0.9
beta_second = 0.95
learn_rate = 0.001
weight_decay = 0.1
epsilon = 1e-08
correct_first = 0.999973438601112
correct_second = 0.99407947077967

BF = jnp.bfloat16
F32 = jnp.float32
MB = 1024 * 1024

GRAY = (0, 1, 3, 2)
CORE, X1, X2, Y = 1, 2, 4, 8
ENC = [(d % 2) | (GRAY[(d // 2) % 4] << 1) | ((d // 8) << 3) for d in range(16)]
DEC = [ENC.index(r) for r in range(16)]
ORDERS = (((X1, Y, X2), (X2, X1, Y)), ((Y, X2, X1), (Y, X2, X1)))
PARTS = 2


def flip(masks):
    return [(d, DEC[ENC[d] ^ masks[d % 2]]) for d in range(16)]


def relative(order, q):
    return (q >> 2 & 1) * order[0] | (q >> 1 & 1) * order[1] | (q & 1) * order[2]


def swap(value, part, step):
    return lax.ppermute(value, "dp", flip([order[step] for order in ORDERS[part]]))


def swap_cores(value):
    return lax.ppermute(value, "dp", flip((CORE, CORE)))


def aligned(index, size):
    return pl.ds(pl.multiple_of(index * size, size), size)


def place(device, part, q):
    first, second = ORDERS[part]
    move = jnp.where(device % 2 == 0, relative(first, q), relative(second, q)) // 2
    x = device // 2 % 4
    moved = ((x ^ (x // 2)) + device // 8 * 4) ^ move
    gray = moved % 4
    return moved - gray + (gray ^ (gray // 2))


def turn(block, device, out_grad, own, other, turned):
    turned[...] = out_grad[...].T
    parity = device[0] % 2
    for i in range(8):
        rows = slice(i * block, (i + 1) * block)
        own[rows, :] = turned[aligned(2 * i + parity, block), :]
        other[rows, :] = turned[aligned(2 * i + 1 - parity, block), :]


def grad_half(start, cuts, block, device, own, got, hidden, hidden_got, outs, lhs, rhs):
    tokens = hidden.shape[0]
    rhs[:tokens, :] = hidden[...]
    rhs[tokens:, :] = hidden_got[...]
    for part in range(PARTS):
        for q in range(4):
            rows = slice(q * block, (q + 1) * block)
            from_rows = aligned(place(device[0], part, start + q), block)
            lhs[part, rows, :tokens] = own[from_rows, :]
            lhs[part, rows, tokens:] = got[from_rows, :]
        outs[part][...] = jnp.dot(
            lhs[part], rhs[:, cuts[part] : cuts[part + 1]], preferred_element_type=F32
        ).astype(BF)


def grad_sent(cuts, block, device, own, got, hidden, hidden_got, *rest):
    grad_half(4, cuts, block, device, own, got, hidden, hidden_got, rest[:PARTS], *rest[PARTS:])


def grad_kept(
    cuts, block, device, own, got, hidden, hidden_got, out_grad, weight, input_grad, *rest
):
    grad_half(0, cuts, block, device, own, got, hidden, hidden_got, rest[:PARTS], *rest[PARTS:])
    input_grad[...] = contract(out_grad, weight)


def summed(terms, rows):
    result = terms[0][rows, :].astype(F32)
    for term in terms[1:]:
        result = result + term[rows, :].astype(F32)
    return result


def add_parts(size, *refs):
    terms, outs = refs[:-PARTS], refs[-PARTS:]
    count = len(terms) // PARTS
    for part in range(PARTS):
        mine = terms[part * count : (part + 1) * count]
        outs[part][...] = summed(mine, slice(size, 2 * size)).astype(BF)


def join_parts(*refs):
    pieces, outs = refs[:-PARTS], refs[-PARTS:]
    count = len(pieces) // PARTS
    for part in range(PARTS):
        row = 0
        for piece in pieces[part * count : (part + 1) * count]:
            outs[part][row : row + piece.shape[0], :] = piece[...]
            row += piece.shape[0]


def adam(cuts, stored, first_moment, second_moment, current, *refs):
    outs = refs[-3 if stored else -PARTS :]
    terms = refs[: -len(outs)]
    count = len(terms) // PARTS
    rows = slice(0, first_moment.shape[0])
    for part in range(PARTS):
        columns = slice(cuts[part], cuts[part + 1])
        grad = summed(terms[part * count : (part + 1) * count], rows)
        first_new = beta_first * first_moment[:, columns] + (1.0 - beta_first) * grad
        second_new = beta_second * second_moment[:, columns] + (1.0 - beta_second) * grad * grad
        update = first_new / correct_first / (jnp.sqrt(second_new / correct_second) + epsilon)
        old = current[:, columns].astype(F32)
        new_weight = (old - learn_rate * (update + weight_decay * old)).astype(BF)
        if stored:
            outs[0][:, columns] = first_new
            outs[1][:, columns] = second_new
            outs[2][:, columns] = new_weight
        else:
            outs[part][...] = new_weight


def product_rows(half, hidden, hidden_got, lhs, upper):
    wanted = 1 - upper if half else upper
    share = 16
    for z in range(8):
        rows = aligned(wanted * 8 + z, share)
        lhs[2 * z * share : (2 * z + 1) * share, :] = hidden[rows, :]
        lhs[(2 * z + 1) * share : (2 * z + 2) * share, :] = hidden_got[rows, :]


def contract(lhs, full):
    return lax.dot_general(
        lhs[...], full[...], (((1,), (1,)), ((), ())), preferred_element_type=F32
    ).astype(BF)


def product_sent(cuts, block, device, upper, hidden, hidden_got, stored, *rest):
    pieces, (out, full, lhs) = rest[:-3], rest[-3:]
    per_part = len(pieces) // PARTS
    for part in range(PARTS):
        columns = slice(cuts[part], cuts[part + 1])
        q = 0
        for ref in pieces[part * per_part : (part + 1) * per_part]:
            for k in range(ref.shape[0] // block):
                to_rows = aligned(place(device[0], part, q), block)
                full[to_rows, columns] = ref[k * block : (k + 1) * block, :]
                q += 1
    product_rows(True, hidden, hidden_got, lhs, upper[0])
    out[...] = contract(lhs, full)


def product_kept(upper, hidden, hidden_got, full, out, lhs):
    product_rows(False, hidden, hidden_got, lhs, upper[0])
    out[...] = contract(lhs, full)


def add_pair(one, two, out):
    out[...] = (one[...].astype(F32) + two[...].astype(F32)).astype(BF)


def add_shares(shares, own, other):
    value = shares[0].astype(F32)
    for source in range(1, shares.shape[0]):
        value = value + shares[source].astype(F32)
    rows = own.shape[0]
    own[...] = value[:rows].astype(BF)
    other[...] = value[rows:].astype(BF)


def spread(block, device, own, got, out):
    parity = device[0] % 2
    mine, theirs = own[...].astype(F32), got[...].astype(F32)
    even = jnp.where(parity == 0, mine, theirs)
    odd = jnp.where(parity == 0, theirs, mine)
    pieces = []
    for i in range(8):
        columns = slice(i * block, (i + 1) * block)
        pieces += [even[:, columns], odd[:, columns]]
    value = jnp.concatenate(pieces, axis=1).astype(BF)
    for t in range(out.shape[0]):
        out[t] = value


def shape(*dims):
    return jax.ShapeDtypeStruct(dims, BF)


def call(kernel, out_shape, scalars, arrays, scratch=(), unread=(), flops=0, limit=16):
    vmem = pl.BlockSpec(memory_space=pltpu.VMEM)
    smem = pl.BlockSpec(memory_space=pltpu.SMEM)
    anywhere = pl.BlockSpec(memory_space=pl.ANY)
    return pl.pallas_call(
        kernel,
        out_shape=out_shape,
        in_specs=[smem] * len(scalars)
        + [anywhere if any(a is u for u in unread) else vmem for a in arrays],
        out_specs=jax.tree.map(lambda _: vmem, out_shape),
        scratch_shapes=[pltpu.VMEM(dims, BF) for dims in scratch],
        compiler_params=pltpu.CompilerParams(vmem_limit_bytes=limit * MB),
        cost_estimate=pl.CostEstimate(
            flops=flops, bytes_accessed=sum(a.size * 2 for a in arrays), transcendentals=0
        ),
    )(*scalars, *arrays)


def shards(hidden, out_grad, weight, first_moment, second_moment, next_hidden):
    block = first_moment.shape[0]
    tokens, units = hidden.shape
    features = out_grad.shape[1]
    cuts = (0, units // 3 * 2, units)
    position = lax.axis_index("dp")
    device = position.reshape(1)
    upper = (lax.axis_index("tensor") // 8).reshape(1)
    sizes = [cuts[p + 1] - cuts[p] for p in range(PARTS)]

    def parts(rows):
        return tuple(shape(rows, size) for size in sizes)

    hidden_got = swap_cores(hidden)
    own, other = call(
        functools.partial(turn, block),
        (shape(features // 2, tokens), shape(features // 2, tokens)),
        [device],
        [out_grad],
        [(features, tokens)],
    )
    got = swap_cores(other)
    scratch = [(PARTS, 4 * block, 2 * tokens), (2 * tokens, units)]
    sent = call(
        functools.partial(grad_sent, cuts, block),
        parts(4 * block),
        [device],
        [own, got, hidden, hidden_got],
        scratch,
        flops=tokens * units * features,
    )
    arrived = [[swap(sent[p], p, 0) for p in range(PARTS)]]
    input_grad, *kept = call(
        functools.partial(grad_kept, cuts, block),
        (shape(tokens, units),) + parts(4 * block),
        [device],
        [own, got, hidden, hidden_got, out_grad, weight],
        scratch,
        flops=3 * tokens * units * features,
        limit=24,
    )
    next_got = swap_cores(next_hidden)
    current = lax.dynamic_slice_in_dim(weight, position * block, block, 1).T

    def terms():
        return [t for p in range(PARTS) for t in [kept[p]] + [a[p] for a in arrived]]

    for step in (1, 2):
        rows = 4 * block >> step
        mine = call(functools.partial(add_parts, rows), parts(rows), [], terms())
        arrived.append([swap(mine[p], p, step) for p in range(PARTS)])

    inputs = [first_moment, second_moment, current] + terms()
    own_weight = call(functools.partial(adam, cuts, False), parts(block), [], inputs)

    pieces = [[own_weight[p]] for p in range(PARTS)]
    joined = own_weight
    for step in (2, 1, 0):
        for p in range(PARTS):
            pieces[p].append(swap(joined[p], p, step))
        if step == 2:
            moments = jax.ShapeDtypeStruct(first_moment.shape, F32)
            first_new, second_new, new_weight = call(
                functools.partial(adam, cuts, True), (moments, moments, shape(block, units)), [], inputs
            )
        if step:
            joined = call(join_parts, parts(8 * block >> step), [], pieces[0] + pieces[1])
    sent_out, full = call(
        functools.partial(product_sent, cuts, block),
        (shape(tokens, features // 2), shape(features // 2, units)),
        [device, upper],
        [next_hidden, next_got, new_weight] + pieces[0] + pieces[1],
        [(tokens, units)],
        [new_weight],
        flops=tokens * units * features,
    )

    across = lax.ppermute(sent_out, "tensor", [(t, (t + 8) % 16) for t in range(16)])
    kept_out = call(
        product_kept,
        shape(tokens, features // 2),
        [upper],
        [next_hidden, next_got, full],
        [(tokens, units)],
        flops=tokens * units * features,
    )
    halves = call(add_pair, shape(tokens, features // 2), [], [kept_out, across])
    shares = lax.all_to_all(
        halves.reshape(8, tokens // 8, features // 2),
        "tensor",
        0,
        0,
        axis_index_groups=[list(range(8)), list(range(8, 16))],
    )
    share = call(add_shares, (shape(16, features // 2),) * 2, [], [shares])
    lacking = swap_cores(share[1])
    copies = call(
        functools.partial(spread, block),
        shape(16, 16, features),
        [device],
        [share[0], lacking],
    )
    next_out = lax.all_to_all(copies, "tensor", 0, 0).reshape(tokens, features)
    return (input_grad, first_new, second_new, new_weight, next_out)


def solution(mesh):
    placed = (
        P("dp", "tensor"),
        P("dp", None),
        P("tensor", None),
        P("dp", "tensor"),
        P("dp", "tensor"),
        P("dp", "tensor"),
    )
    return jax.shard_map(
        shards,
        mesh=mesh,
        in_specs=placed,
        out_specs=(
            P("dp", "tensor"),
            P("dp", "tensor"),
            P("dp", "tensor"),
            P("dp", "tensor"),
            P("dp", None),
        ),
        check_vma=False,
    )
```

```python
import functools

import jax
import jax.numpy as jnp
import numpy as np
from jax import lax
from jax.experimental import pallas as pl
from jax.experimental.pallas import tpu as pltpu
from jax.sharding import PartitionSpec as P

beta_first = 0.9
beta_second = 0.95
learn_rate = 0.001
weight_decay = 0.1
epsilon = 1e-08
correct_first = 0.999973438601112
correct_second = 0.99407947077967

BF = jnp.bfloat16
F32 = jnp.float32
MB = 1024 * 1024

GRAY = (0, 1, 3, 2)
CORE, X1, X2, Y = 1, 2, 4, 8
ENC = [(d % 2) | (GRAY[(d // 2) % 4] << 1) | ((d // 8) << 3) for d in range(16)]
DEC = [ENC.index(r) for r in range(16)]
ORDERS = (((X1, Y, X2), (X2, X1, Y)), ((Y, X2, X1), (Y, X2, X1)))
PARTS = 2


def flip(masks):
    return [(d, DEC[ENC[d] ^ masks[d % 2]]) for d in range(16)]


def relative(order, q):
    return (q >> 2 & 1) * order[0] | (q >> 1 & 1) * order[1] | (q & 1) * order[2]


def swap(value, part, step):
    return lax.ppermute(value, "dp", flip([order[step] for order in ORDERS[part]]))


def swap_cores(value):
    return lax.ppermute(value, "dp", flip((CORE, CORE)))


def aligned(index, size):
    return pl.ds(pl.multiple_of(index * size, size), size)


def place(device, part, q):
    first, second = ORDERS[part]
    move = jnp.where(device % 2 == 0, relative(first, q), relative(second, q)) // 2
    x = device // 2 % 4
    moved = ((x ^ (x // 2)) + device // 8 * 4) ^ move
    gray = moved % 4
    return moved - gray + (gray ^ (gray // 2))


def turn(block, device, out_grad, own, other, turned):
    turned[...] = out_grad[...].T
    parity = device[0] % 2
    for i in range(8):
        rows = slice(i * block, (i + 1) * block)
        own[rows, :] = turned[aligned(2 * i + parity, block), :]
        other[rows, :] = turned[aligned(2 * i + 1 - parity, block), :]


def grad_half(start, cuts, block, device, own, got, hidden, hidden_got, outs, lhs, rhs):
    tokens = hidden.shape[0]
    rhs[:tokens, :] = hidden[...]
    rhs[tokens:, :] = hidden_got[...]
    for part in range(PARTS):
        for q in range(4):
            rows = slice(q * block, (q + 1) * block)
            from_rows = aligned(place(device[0], part, start + q), block)
            lhs[part, rows, :tokens] = own[from_rows, :]
            lhs[part, rows, tokens:] = got[from_rows, :]
        outs[part][...] = jnp.dot(
            lhs[part], rhs[:, cuts[part] : cuts[part + 1]], preferred_element_type=F32
        ).astype(BF)


def grad_sent(cuts, block, device, own, got, hidden, hidden_got, *rest):
    grad_half(4, cuts, block, device, own, got, hidden, hidden_got, rest[:PARTS], *rest[PARTS:])


def grad_kept(
    cuts, block, device, tensor, own, got, hidden, hidden_got, out_grad, weight, nexts, nexts_got, *rest
):
    input_grad, rows_one, rows_two = rest[:3]
    rest = rest[3:]
    grad_half(0, cuts, block, device, own, got, hidden, hidden_got, rest[:PARTS], *rest[PARTS:])
    input_grad[...] = contract(out_grad, weight)
    for place_one, place_two, owner in owners(tensor[0], 1):
        rows = aligned(owner, 16)
        for out, at in ((rows_one, place_one), (rows_two, place_two)):
            out[32 * at : 32 * at + 16, :] = nexts[rows, :]
            out[32 * at + 16 : 32 * at + 32, :] = nexts_got[rows, :]


def owners(tensor, sign):
    upper, low, quarter = tensor // 8, tensor % 2, tensor % 8 // 2
    for y in range(2):
        for b in range(2):
            for k in range(4):
                owner = (upper + y) % 2 * 8 + (quarter + sign * k + 4) % 4 * 2 + (low + b) % 2
                yield y * 8 + b * 4 + k, b * 8 + y * 4 + k, owner


def total(terms, rows):
    result = terms[0][rows, :].astype(F32)
    for term in terms[1:]:
        result = result + term[rows, :].astype(F32)
    return result


def add_parts(size, *refs):
    terms, outs = refs[: -2 * PARTS], refs[-2 * PARTS :]
    for part in range(PARTS):
        mine = terms[2 * part : 2 * part + 2]
        outs[part][...] = total(mine, slice(size, 2 * size)).astype(BF)
        outs[PARTS + part][...] = total(mine, slice(0, size))


def add_parts_and_cast(size, current, *refs):
    add_parts(size, *refs[:-1])
    refs[-1][...] = current[...].astype(F32)


def join_parts(*refs):
    for part in range(PARTS):
        upper, lower = refs[2 * part : 2 * part + 2]
        out = refs[2 * PARTS + part]
        rows = upper.shape[0]
        out[:rows, :] = upper[...]
        out[rows:, :] = lower[...]


def decay(first_moment, second_moment, first, second):
    first[...] = beta_first * first_moment[...]
    second[...] = beta_second * second_moment[...]


def adam(cuts, first, second, current, *refs):
    terms, outs = refs[: 2 * PARTS], refs[2 * PARTS :]
    for part in range(PARTS):
        columns = slice(cuts[part], cuts[part + 1])
        grad = total(terms[2 * part : 2 * part + 2], slice(None))
        first_new = first[:, columns] + (1.0 - beta_first) * grad
        second_new = second[:, columns] + (1.0 - beta_second) * grad * grad
        update = first_new / correct_first / (jnp.sqrt(second_new / correct_second) + epsilon)
        old = current[:, columns]
        new_weight = (old - learn_rate * (update + weight_decay * old)).astype(BF)
        outs[part][...] = new_weight
        outs[PARTS][:, columns] = first_new
        outs[PARTS + 1][:, columns] = second_new
        outs[PARTS + 2][:, columns] = new_weight


def contract(one, two):
    return lax.dot_general(
        one[...], two[...], (((1,), (1,)), ((), ())), preferred_element_type=F32
    ).astype(BF)


def product_sent(cuts, block, cut, device, rows_one, rows_two, *rest):
    pieces, (out_one, out_two, full) = rest[: 2 * PARTS], rest[2 * PARTS :]
    for part in range(PARTS):
        columns = slice(cuts[part], cuts[part + 1])
        for q in range(8):
            ref = pieces[2 * part + q // 4]
            to_rows = aligned(place(device[0], part, q), block)
            full[to_rows, columns] = ref[q % 4 * block : (q % 4 + 1) * block, :]
    half = rows_one.shape[0] // 2
    out_one[...] = contract(rows_one.at[half:], full.at[:cut])
    out_two[...] = contract(rows_two.at[half:], full.at[cut:])


def product_kept(cut, rows_one, rows_two, full, out_one, out_two):
    half = rows_one.shape[0] // 2
    out_one[...] = contract(rows_one.at[:half], full.at[:cut])
    out_two[...] = contract(rows_two.at[:half], full.at[cut:])


def add_quarters(cut, *refs):
    terms, outs = refs[: 2 * PARTS], refs[2 * PARTS :]
    for part, columns in enumerate((slice(0, cut), slice(cut, None))):
        for k in range(4):
            rows = total(terms[2 * part : 2 * part + 2], slice(32 * k, 32 * k + 32))
            outs[k][:, columns] = rows.astype(outs[k].dtype)


def add_shares(one, two, three, four, own, other):
    value = total((one, two, three, four), slice(None))
    own[...] = value[:16].astype(BF)
    other[...] = value[16:].astype(BF)


def weave(block, device, own, got, out):
    parity = device[0] % 2
    mine, theirs = own[...].astype(F32), got[...].astype(F32)
    even = jnp.where(parity == 0, mine, theirs)
    odd = jnp.where(parity == 0, theirs, mine)
    pieces = []
    for i in range(8):
        columns = slice(i * block, (i + 1) * block)
        pieces += [even[:, columns], odd[:, columns]]
    out[...] = jnp.concatenate(pieces, axis=1).astype(BF)


def join_quarters(cut, *refs):
    quarters, outs = refs[:4], refs[4:]
    for part, columns in enumerate((slice(0, cut), slice(cut, None))):
        for k in range(4):
            outs[part][16 * k : 16 * k + 16, :] = quarters[k][:, columns]


def place_rows(cut, tensor, one, one_got, two, two_got, out):
    for place_one, place_two, owner in owners(tensor[0], -1):
        rows = aligned(owner, 16)
        for place_in, refs, columns in (
            (place_one, (one, one_got), slice(0, cut)),
            (place_two, (two, two_got), slice(cut, None)),
        ):
            at = place_in % 8 * 16
            out[rows, columns] = refs[place_in // 8][at : at + 16, :]


def shape(*dims, dtype=BF):
    return jax.ShapeDtypeStruct(dims, dtype)


def call(kernel, out_shape, scalars, arrays, scratch=(), flops=0, limit=16):
    vmem = pl.BlockSpec(memory_space=pltpu.VMEM)
    smem = pl.BlockSpec(memory_space=pltpu.SMEM)
    return pl.pallas_call(
        kernel,
        out_shape=out_shape,
        in_specs=[smem] * len(scalars) + [vmem] * len(arrays),
        out_specs=jax.tree.map(lambda _: vmem, out_shape),
        scratch_shapes=[pltpu.VMEM(dims, BF) for dims in scratch],
        compiler_params=pltpu.CompilerParams(vmem_limit_bytes=limit * MB),
        cost_estimate=pl.CostEstimate(
            flops=flops, bytes_accessed=sum(a.size * 2 for a in arrays), transcendentals=0
        ),
    )(*scalars, *arrays)


def move(value, function):
    return lax.ppermute(value, "tensor", [(t, function(t)) for t in range(16)])


def swap_upper(value):
    return move(value, lambda t: (t + 8) % 16)


def swap_low(value):
    return move(value, lambda t: t ^ 1)


def shift(value, quarters):
    return move(value, lambda t: t // 8 * 8 + (t + 2 * quarters) % 8)


def shards(hidden, out_grad, weight, first_moment, second_moment, next_hidden):
    block = first_moment.shape[0]
    tokens, units = hidden.shape
    features = out_grad.shape[1]
    cuts = (0, units // 3 * 2, units)
    sizes = [cuts[p + 1] - cuts[p] for p in range(PARTS)]
    position = lax.axis_index("dp")
    device = position.reshape(1)
    tensor = lax.axis_index("tensor").reshape(1)
    product = tokens * units * features

    def parts(rows, dtype=BF):
        return tuple(shape(rows, size, dtype=dtype) for size in sizes)

    hidden_got = swap_cores(hidden)
    own, other = call(
        functools.partial(turn, block),
        (shape(features // 2, tokens), shape(features // 2, tokens)),
        [device],
        [out_grad],
        [(features, tokens)],
    )
    got = swap_cores(other)
    scratch = [(PARTS, 4 * block, 2 * tokens), (2 * tokens, units)]
    sent = call(
        functools.partial(grad_sent, cuts, block),
        parts(4 * block),
        [device],
        [own, got, hidden, hidden_got],
        scratch,
        flops=product,
    )
    arrived = [swap(sent[p], p, 0) for p in range(PARTS)]
    next_got = swap_cores(next_hidden)
    input_grad, rows_one, rows_two, *kept = call(
        functools.partial(grad_kept, cuts, block),
        (shape(tokens, units), shape(2 * tokens, units), shape(2 * tokens, units)) + parts(4 * block),
        [device, tensor],
        [own, got, hidden, hidden_got, out_grad, weight, next_hidden, next_got],
        scratch,
        flops=3 * product,
        limit=28,
    )

    def pairs(upper, lower):
        return [array for p in range(PARTS) for array in (upper[p], lower[p])]

    rows = 2 * block
    sums = call(
        functools.partial(add_parts, rows), parts(rows) + parts(rows, F32), [], pairs(kept, arrived)
    )
    arrived = [swap(sums[p], p, 1) for p in range(PARTS)]
    current = lax.dynamic_slice_in_dim(weight, position * block, block, 1).T
    moments = shape(block, units, dtype=F32)
    *sums, current = call(
        functools.partial(add_parts_and_cast, block),
        parts(block) + parts(block, F32) + (moments,),
        [],
        [current] + pairs(sums[PARTS:], arrived),
    )
    arrived = [swap(sums[p], p, 2) for p in range(PARTS)]
    first, second = call(decay, (moments, moments), [], [first_moment, second_moment])
    *held, first_new, second_new, new_weight = call(
        functools.partial(adam, cuts),
        parts(block) + (moments, moments, shape(block, units)),
        [],
        [first, second, current] + pairs(sums[PARTS:], arrived),
    )

    for step in (2, 1, 0):
        arrived = [swap(held[p], p, step) for p in range(PARTS)]
        if step:
            held = call(join_parts, parts(8 * block >> step), [], pairs(held, arrived))

    wide = features // 2
    cut = wide // 9 * 5
    half = (shape(tokens, cut), shape(tokens, wide - cut))
    sent_one, sent_two, full = call(
        functools.partial(product_sent, cuts, block, cut),
        half + (shape(wide, units),),
        [device],
        [rows_one, rows_two] + pairs(held, arrived),
        flops=product,
    )
    arrived = [swap_upper(sent_one), swap_low(sent_two)]
    kept = call(
        functools.partial(product_kept, cut), half, [], [rows_one, rows_two, full], flops=product
    )
    rows = tokens // 2
    sums = call(
        functools.partial(add_parts, rows),
        tuple(shape(rows, w, dtype=d) for d in (BF, F32) for w in (cut, wide - cut)),
        [],
        pairs(kept, arrived),
    )
    arrived = [swap_low(sums[0]), swap_upper(sums[1])]
    quarters = call(
        functools.partial(add_quarters, cut),
        (shape(32, wide, dtype=F32),) + (shape(32, wide),) * 3,
        [],
        pairs(sums[2:], arrived),
    )
    share, lacking = call(
        add_shares,
        (shape(16, wide), shape(16, wide)),
        [],
        [quarters[0]] + [shift(quarters[k], k) for k in (2, 1, 3)],
    )
    value = call(
        functools.partial(weave, block),
        shape(16, features),
        [device],
        [share, swap_cores(lacking)],
    )

    cut = features // 9 * 5
    widths = (cut, features - cut)
    others = {k: shift(value, k) for k in (2, 1, 3)}
    one, two = call(
        functools.partial(join_quarters, cut),
        tuple(shape(64, w) for w in widths),
        [],
        [value] + [others[k] for k in (1, 2, 3)],
    )
    arrived = [swap_low(one), swap_upper(two)]
    one, two = call(
        join_parts, tuple(shape(128, w) for w in widths), [], pairs((one, two), arrived)
    )
    arrived = [swap_upper(one), swap_low(two)]
    next_out = call(
        functools.partial(place_rows, cut),
        shape(tokens, features),
        [tensor],
        pairs((one, two), arrived),
    )
    return (input_grad, first_new, second_new, new_weight, next_out)


def solution(mesh):
    placed = (
        P("dp", "tensor"),
        P("dp", None),
        P("tensor", None),
        P("dp", "tensor"),
        P("dp", "tensor"),
        P("dp", "tensor"),
    )
    return jax.shard_map(
        shards,
        mesh=mesh,
        in_specs=placed,
        out_specs=(
            P("dp", "tensor"),
            P("dp", "tensor"),
            P("dp", "tensor"),
            P("dp", "tensor"),
            P("dp", None),
        ),
        check_vma=False,
    )
```

```python
import functools

import jax
import jax.numpy as jnp
import numpy as np
from jax import lax
from jax.experimental import pallas as pl
from jax.experimental.pallas import tpu as pltpu
from jax.sharding import PartitionSpec as P

beta_first = 0.9
beta_second = 0.95
learn_rate = 0.001
weight_decay = 0.1
epsilon = 1e-08
correct_first = 0.999973438601112
correct_second = 0.99407947077967

BF = jnp.bfloat16
F32 = jnp.float32
MB = 1024 * 1024

GRAY = (0, 1, 3, 2)
CORE, X1, X2, Y = 1, 2, 4, 8
ENC = [(d % 2) | (GRAY[(d // 2) % 4] << 1) | ((d // 8) << 3) for d in range(16)]
DEC = [ENC.index(r) for r in range(16)]
ORDERS = (((X1, Y, X2), (X2, X1, Y)), ((Y, X2, X1), (Y, X2, X1)))
PARTS = 2


def flip(masks):
    return [(d, DEC[ENC[d] ^ masks[d % 2]]) for d in range(16)]


def relative(order, q):
    return (q >> 2 & 1) * order[0] | (q >> 1 & 1) * order[1] | (q & 1) * order[2]


def swap(value, part, step):
    return lax.ppermute(value, "dp", flip([order[step] for order in ORDERS[part]]))


def swap_cores(value):
    return lax.ppermute(value, "dp", flip((CORE, CORE)))


def aligned(index, size):
    return pl.ds(pl.multiple_of(index * size, size), size)


def place(device, part, q):
    first, second = ORDERS[part]
    move = jnp.where(device % 2 == 0, relative(first, q), relative(second, q)) // 2
    x = device // 2 % 4
    moved = ((x ^ (x // 2)) + device // 8 * 4) ^ move
    gray = moved % 4
    return moved - gray + (gray ^ (gray // 2))


def turn(block, index, out_grad, own, other, turned):
    turned[...] = out_grad[...].T
    parity = index[0] // 16 % 2
    for i in range(8):
        rows = slice(i * block, (i + 1) * block)
        own[rows, :] = turned[aligned(2 * i + parity, block), :]
        other[rows, :] = turned[aligned(2 * i + 1 - parity, block), :]


def grad_half(start, cuts, block, index, own, got, hidden, hidden_got, outs, lhs, rhs):
    tokens = hidden.shape[0]
    rhs[:tokens, :] = hidden[...]
    rhs[tokens:, :] = hidden_got[...]
    for part in range(PARTS):
        for q in range(4):
            rows = slice(q * block, (q + 1) * block)
            from_rows = aligned(place(index[0] // 16, part, start + q), block)
            lhs[part, rows, :tokens] = own[from_rows, :]
            lhs[part, rows, tokens:] = got[from_rows, :]
        outs[part][...] = jnp.dot(
            lhs[part], rhs[:, cuts[part] : cuts[part + 1]], preferred_element_type=F32
        ).astype(BF)


def grad_sent(cuts, block, index, own, got, hidden, hidden_got, *rest):
    grad_half(4, cuts, block, index, own, got, hidden, hidden_got, rest[:PARTS], *rest[PARTS:])


def grad_kept(
    cuts, block, index, own, got, hidden, hidden_got, out_grad, weight, nexts, nexts_got, *rest
):
    input_grad, rows_one, rows_two, current = rest[:4]
    rest, turned = rest[4:-1], rest[-1]
    grad_half(0, cuts, block, index, own, got, hidden, hidden_got, rest[:PARTS], *rest[PARTS:])
    input_grad[...] = contract(out_grad, weight)
    first = index[0] // 16 * block
    columns = pl.ds(pl.multiple_of(first // 128 * 128, 128), turned.shape[0])
    turned[...] = weight[:, columns].T
    current[...] = turned[pl.ds(pl.multiple_of(first % 128, 16), block), :].astype(F32)
    for place_one, place_two, owner in owners(index[0] % 16, 1):
        rows = aligned(owner, 16)
        for out, at in ((rows_one, place_one), (rows_two, place_two)):
            out[32 * at : 32 * at + 16, :] = nexts[rows, :]
            out[32 * at + 16 : 32 * at + 32, :] = nexts_got[rows, :]


def owners(tensor, sign):
    upper, low, quarter = tensor // 8, tensor % 2, tensor % 8 // 2
    for y in range(2):
        for b in range(2):
            for k in range(4):
                owner = (upper + y) % 2 * 8 + (quarter + sign * k + 4) % 4 * 2 + (low + b) % 2
                yield y * 8 + b * 4 + k, b * 8 + y * 4 + k, owner


def total(terms, rows):
    result = terms[0][rows, :].astype(F32)
    for term in terms[1:]:
        result = result + term[rows, :].astype(F32)
    return result


def add_parts(size, *refs):
    terms, outs = refs[: -2 * PARTS], refs[-2 * PARTS :]
    for part in range(PARTS):
        mine = terms[2 * part : 2 * part + 2]
        outs[part][...] = total(mine, slice(size, 2 * size)).astype(BF)
        outs[PARTS + part][...] = total(mine, slice(0, size))


def join_parts(*refs):
    for part in range(PARTS):
        upper, lower = refs[2 * part : 2 * part + 2]
        out = refs[2 * PARTS + part]
        rows = upper.shape[0]
        out[:rows, :] = upper[...]
        out[rows:, :] = lower[...]


def adam(cuts, first_moment, second_moment, current, *refs):
    terms, outs = refs[: 2 * PARTS], refs[2 * PARTS :]
    for part in range(PARTS):
        columns = slice(cuts[part], cuts[part + 1])
        grad = total(terms[2 * part : 2 * part + 2], slice(None))
        first_new = beta_first * first_moment[:, columns] + (1.0 - beta_first) * grad
        second_new = beta_second * second_moment[:, columns] + (1.0 - beta_second) * grad * grad
        update = first_new / correct_first / (jnp.sqrt(second_new / correct_second) + epsilon)
        old = current[:, columns]
        new_weight = (old - learn_rate * (update + weight_decay * old)).astype(BF)
        outs[part][...] = new_weight
        outs[PARTS][:, columns] = first_new
        outs[PARTS + 1][:, columns] = second_new
        outs[PARTS + 2][:, columns] = new_weight


def contract(one, two):
    return lax.dot_general(
        one[...], two[...], (((1,), (1,)), ((), ())), preferred_element_type=F32
    ).astype(BF)


def product_sent(cuts, block, cut, index, rows_one, rows_two, *rest):
    pieces, (out_one, out_two, full) = rest[: 2 * PARTS], rest[2 * PARTS :]
    for part in range(PARTS):
        columns = slice(cuts[part], cuts[part + 1])
        for q in range(8):
            ref = pieces[2 * part + q // 4]
            to_rows = aligned(place(index[0] // 16, part, q), block)
            full[to_rows, columns] = ref[q % 4 * block : (q % 4 + 1) * block, :]
    half = rows_one.shape[0] // 2
    out_one[...] = contract(rows_one.at[half:], full.at[:cut])
    out_two[...] = contract(rows_two.at[half:], full.at[cut:])


def product_kept(cut, rows_one, rows_two, full, out_one, out_two):
    half = rows_one.shape[0] // 2
    out_one[...] = contract(rows_one.at[:half], full.at[:cut])
    out_two[...] = contract(rows_two.at[:half], full.at[cut:])


def add_quarters(cut, *refs):
    terms, outs = refs[: 2 * PARTS], refs[2 * PARTS :]
    for part, columns in enumerate((slice(0, cut), slice(cut, None))):
        for k in range(4):
            rows = total(terms[2 * part : 2 * part + 2], slice(32 * k, 32 * k + 32))
            outs[k][:, columns] = rows.astype(outs[k].dtype)


def add_shares(one, two, three, four, own, other):
    value = total((one, two, three, four), slice(None))
    own[...] = value[:16].astype(BF)
    other[...] = value[16:].astype(BF)


def weave(block, index, own, got, out):
    parity = index[0] // 16 % 2
    mine, theirs = own[...].astype(F32), got[...].astype(F32)
    even = jnp.where(parity == 0, mine, theirs)
    odd = jnp.where(parity == 0, theirs, mine)
    pieces = []
    for i in range(8):
        columns = slice(i * block, (i + 1) * block)
        pieces += [even[:, columns], odd[:, columns]]
    out[...] = jnp.concatenate(pieces, axis=1).astype(BF)


def join_quarters(cut, *refs):
    quarters, outs = refs[:4], refs[4:]
    for part, columns in enumerate((slice(0, cut), slice(cut, None))):
        for k in range(4):
            outs[part][16 * k : 16 * k + 16, :] = quarters[k][:, columns]


def place_rows(cut, index, one, one_got, two, two_got, out):
    for place_one, place_two, owner in owners(index[0] % 16, -1):
        rows = aligned(owner, 16)
        for place_in, refs, columns in (
            (place_one, (one, one_got), slice(0, cut)),
            (place_two, (two, two_got), slice(cut, None)),
        ):
            at = place_in % 8 * 16
            out[rows, columns] = refs[place_in // 8][at : at + 16, :]


def shape(*dims, dtype=BF):
    return jax.ShapeDtypeStruct(dims, dtype)


def call(kernel, out_shape, scalars, arrays, scratch=(), flops=0, limit=16):
    vmem = pl.BlockSpec(memory_space=pltpu.VMEM)
    smem = pl.BlockSpec(memory_space=pltpu.SMEM)
    return pl.pallas_call(
        kernel,
        out_shape=out_shape,
        in_specs=[smem] * len(scalars) + [vmem] * len(arrays),
        out_specs=jax.tree.map(lambda _: vmem, out_shape),
        scratch_shapes=[pltpu.VMEM(dims, BF) for dims in scratch],
        compiler_params=pltpu.CompilerParams(vmem_limit_bytes=limit * MB),
        cost_estimate=pl.CostEstimate(
            flops=flops, bytes_accessed=sum(a.size * 2 for a in arrays), transcendentals=0
        ),
    )(*scalars, *arrays)


def move(value, function):
    return lax.ppermute(value, "tensor", [(t, function(t)) for t in range(16)])


def swap_upper(value):
    return move(value, lambda t: (t + 8) % 16)


def swap_low(value):
    return move(value, lambda t: t ^ 1)


def shift(value, quarters):
    return move(value, lambda t: t // 8 * 8 + (t + 2 * quarters) % 8)


def shards(hidden, out_grad, weight, first_moment, second_moment, next_hidden):
    block = first_moment.shape[0]
    tokens, units = hidden.shape
    features = out_grad.shape[1]
    cuts = (0, units // 3 * 2, units)
    sizes = [cuts[p + 1] - cuts[p] for p in range(PARTS)]
    index = lax.axis_index(("dp", "tensor")).reshape(1)
    product = tokens * units * features

    def parts(rows, dtype=BF):
        return tuple(shape(rows, size, dtype=dtype) for size in sizes)

    hidden_got = swap_cores(hidden)
    own, other = call(
        functools.partial(turn, block),
        (shape(features // 2, tokens), shape(features // 2, tokens)),
        [index],
        [out_grad],
        [(features, tokens)],
    )
    got = swap_cores(other)
    scratch = [(PARTS, 4 * block, 2 * tokens), (2 * tokens, units)]
    sent = call(
        functools.partial(grad_sent, cuts, block),
        parts(4 * block),
        [index],
        [own, got, hidden, hidden_got],
        scratch,
        flops=product,
    )
    arrived = [swap(sent[p], p, 0) for p in range(PARTS)]
    next_got = swap_cores(next_hidden)
    moments = shape(block, units, dtype=F32)
    input_grad, rows_one, rows_two, current, *kept = call(
        functools.partial(grad_kept, cuts, block),
        (shape(tokens, units), shape(2 * tokens, units), shape(2 * tokens, units), moments)
        + parts(4 * block),
        [index],
        [own, got, hidden, hidden_got, out_grad, weight, next_hidden, next_got],
        scratch + [(256, units)],
        flops=3 * product,
        limit=28,
    )

    def pairs(upper, lower):
        return [array for p in range(PARTS) for array in (upper[p], lower[p])]

    for step in (1, 2):
        rows = 4 * block >> step
        sums = call(
            functools.partial(add_parts, rows),
            parts(rows) + parts(rows, F32),
            [],
            pairs(kept, arrived),
        )
        arrived, kept = [swap(sums[p], p, step) for p in range(PARTS)], sums[PARTS:]
    *held, first_new, second_new, new_weight = call(
        functools.partial(adam, cuts),
        parts(block) + (moments, moments, shape(block, units)),
        [],
        [first_moment, second_moment, current] + pairs(kept, arrived),
    )

    for step in (2, 1, 0):
        arrived = [swap(held[p], p, step) for p in range(PARTS)]
        if step:
            held = call(join_parts, parts(8 * block >> step), [], pairs(held, arrived))

    wide = features // 2
    cut = wide // 9 * 5
    half = (shape(tokens, cut), shape(tokens, wide - cut))
    sent_one, sent_two, full = call(
        functools.partial(product_sent, cuts, block, cut),
        half + (shape(wide, units),),
        [index],
        [rows_one, rows_two] + pairs(held, arrived),
        flops=product,
    )
    arrived = [swap_upper(sent_one), swap_low(sent_two)]
    kept = call(
        functools.partial(product_kept, cut), half, [], [rows_one, rows_two, full], flops=product
    )
    rows = tokens // 2
    sums = call(
        functools.partial(add_parts, rows),
        tuple(shape(rows, w, dtype=d) for d in (BF, F32) for w in (cut, wide - cut)),
        [],
        pairs(kept, arrived),
    )
    arrived = [swap_low(sums[0]), swap_upper(sums[1])]
    quarters = call(
        functools.partial(add_quarters, cut),
        (shape(32, wide, dtype=F32),) + (shape(32, wide),) * 3,
        [],
        pairs(sums[2:], arrived),
    )
    share, lacking = call(
        add_shares,
        (shape(16, wide), shape(16, wide)),
        [],
        [quarters[0]] + [shift(quarters[k], k) for k in (2, 1, 3)],
    )
    value = call(
        functools.partial(weave, block),
        shape(16, features),
        [index],
        [share, swap_cores(lacking)],
    )

    cut = features // 9 * 5
    widths = (cut, features - cut)
    others = {k: shift(value, k) for k in (2, 1, 3)}
    one, two = call(
        functools.partial(join_quarters, cut),
        tuple(shape(64, w) for w in widths),
        [],
        [value] + [others[k] for k in (1, 2, 3)],
    )
    arrived = [swap_low(one), swap_upper(two)]
    one, two = call(
        join_parts, tuple(shape(128, w) for w in widths), [], pairs((one, two), arrived)
    )
    arrived = [swap_upper(one), swap_low(two)]
    next_out = call(
        functools.partial(place_rows, cut),
        shape(tokens, features),
        [index],
        pairs((one, two), arrived),
    )
    return (input_grad, first_new, second_new, new_weight, next_out)


def solution(mesh):
    placed = (
        P("dp", "tensor"),
        P("dp", None),
        P("tensor", None),
        P("dp", "tensor"),
        P("dp", "tensor"),
        P("dp", "tensor"),
    )
    return jax.shard_map(
        shards,
        mesh=mesh,
        in_specs=placed,
        out_specs=(
            P("dp", "tensor"),
            P("dp", "tensor"),
            P("dp", "tensor"),
            P("dp", "tensor"),
            P("dp", None),
        ),
        check_vma=False,
    )
```

```python
import functools

import jax
import jax.numpy as jnp
import numpy as np
from jax import lax
from jax.experimental import pallas as pl
from jax.experimental.pallas import tpu as pltpu
from jax.sharding import PartitionSpec as P

beta_first = 0.9
beta_second = 0.95
learn_rate = 0.001
weight_decay = 0.1
epsilon = 1e-08
correct_first = 0.999973438601112
correct_second = 0.99407947077967

BF = jnp.bfloat16
F32 = jnp.float32
MB = 1024 * 1024

GRAY = (0, 1, 3, 2)
CORE, X1, X2, Y = 1, 2, 4, 8
ENC = [(d % 2) | (GRAY[(d // 2) % 4] << 1) | ((d // 8) << 3) for d in range(16)]
DEC = [ENC.index(r) for r in range(16)]
ORDERS = (((X1, Y, X2), (X2, X1, Y)), ((Y, X2, X1), (Y, X2, X1)))
PARTS = 2


def flip(masks):
    return [(d, DEC[ENC[d] ^ masks[d % 2]]) for d in range(16)]


def relative(order, q):
    return (q >> 2 & 1) * order[0] | (q >> 1 & 1) * order[1] | (q & 1) * order[2]


def swap(value, part, step):
    return lax.ppermute(value, "dp", flip([order[step] for order in ORDERS[part]]))


def swap_cores(value):
    return lax.ppermute(value, "dp", flip((CORE, CORE)))


def aligned(index, size):
    return pl.ds(pl.multiple_of(index * size, size), size)


def place(device, part, q):
    first, second = ORDERS[part]
    move = jnp.where(device % 2 == 0, relative(first, q), relative(second, q)) // 2
    x = device // 2 % 4
    moved = ((x ^ (x // 2)) + device // 8 * 4) ^ move
    gray = moved % 4
    return moved - gray + (gray ^ (gray // 2))


def turn(block, index, out_grad, own, other, turned):
    turned[...] = out_grad[...].T
    parity = index[0] // 16 % 2
    for i in range(8):
        rows = slice(i * block, (i + 1) * block)
        own[rows, :] = turned[aligned(2 * i + parity, block), :]
        other[rows, :] = turned[aligned(2 * i + 1 - parity, block), :]


def grad_half(start, cuts, block, index, own, got, hidden, hidden_got, outs, lhs, rhs):
    tokens = hidden.shape[0]
    rhs[:tokens, :] = hidden[...]
    rhs[tokens:, :] = hidden_got[...]
    for part in range(PARTS):
        for q in range(4):
            rows = slice(q * block, (q + 1) * block)
            from_rows = aligned(place(index[0] // 16, part, start + q), block)
            lhs[part, rows, :tokens] = own[from_rows, :]
            lhs[part, rows, tokens:] = got[from_rows, :]
        outs[part][...] = jnp.dot(
            lhs[part], rhs[:, cuts[part] : cuts[part + 1]], preferred_element_type=F32
        ).astype(BF)


def grad_sent(cuts, block, index, own, got, hidden, hidden_got, *rest):
    grad_half(4, cuts, block, index, own, got, hidden, hidden_got, rest[:PARTS], *rest[PARTS:])


def grad_kept(
    cuts, block, index, own, got, hidden, hidden_got, out_grad, weight, nexts, nexts_got, *rest
):
    input_grad, arranged, current = rest[:3]
    rest, turned = rest[3:-1], rest[-1]
    grad_half(0, cuts, block, index, own, got, hidden, hidden_got, rest[:PARTS], *rest[PARTS:])
    input_grad[...] = contract(out_grad, weight)
    first = index[0] // 16 * block
    columns = pl.ds(pl.multiple_of(first // 128 * 128, 128), turned.shape[0])
    turned[...] = weight[:, columns].T
    current[...] = turned[pl.ds(pl.multiple_of(first % 128, 16), block), :].astype(F32)
    for at, owner in owners(index[0], 1):
        rows = aligned(owner, 16)
        arranged[32 * at : 32 * at + 16, :] = nexts[rows, :]
        arranged[32 * at + 16 : 32 * at + 32, :] = nexts_got[rows, :]


def owners(index, sign):
    upper, low, quarter, core = index % 16 // 8, index % 2, index % 8 // 2, index // 16 % 2
    for one in range(2):
        for two in range(2):
            y, b = one + core * (two - one), two + core * (one - two)
            for k in range(4):
                owner = (upper + y) % 2 * 8 + (quarter + sign * k + 4) % 4 * 2 + (low + b) % 2
                yield one * 8 + two * 4 + k, owner


def total(terms, rows):
    result = terms[0][rows, :].astype(F32)
    for term in terms[1:]:
        result = result + term[rows, :].astype(F32)
    return result


def add_parts(size, *refs):
    parts = len(refs) // 4
    terms, outs = refs[: 2 * parts], refs[2 * parts :]
    for part in range(parts):
        mine = terms[2 * part : 2 * part + 2]
        outs[part][...] = total(mine, slice(size, 2 * size)).astype(BF)
        outs[parts + part][...] = total(mine, slice(0, size))


def join_parts(*refs):
    parts = len(refs) // 3
    for part in range(parts):
        upper, lower = refs[2 * part : 2 * part + 2]
        out = refs[2 * parts + part]
        rows = upper.shape[0]
        out[:rows, :] = upper[...]
        out[rows:, :] = lower[...]


def adam(cuts, first_moment, second_moment, current, *refs):
    terms, outs = refs[: 2 * PARTS], refs[2 * PARTS :]
    for part in range(PARTS):
        columns = slice(cuts[part], cuts[part + 1])
        grad = total(terms[2 * part : 2 * part + 2], slice(None))
        first_new = beta_first * first_moment[:, columns] + (1.0 - beta_first) * grad
        second_new = beta_second * second_moment[:, columns] + (1.0 - beta_second) * grad * grad
        update = first_new / correct_first / (jnp.sqrt(second_new / correct_second) + epsilon)
        old = current[:, columns]
        new_weight = (old - learn_rate * (update + weight_decay * old)).astype(BF)
        outs[part][...] = new_weight
        outs[PARTS][:, columns] = first_new
        outs[PARTS + 1][:, columns] = second_new
        outs[PARTS + 2][:, columns] = new_weight


def contract(one, two):
    return lax.dot_general(
        one[...], two[...], (((1,), (1,)), ((), ())), preferred_element_type=F32
    ).astype(BF)


def product_sent(cuts, block, index, arranged, *rest):
    pieces, (out, full) = rest[: 2 * PARTS], rest[2 * PARTS :]
    for part in range(PARTS):
        columns = slice(cuts[part], cuts[part + 1])
        for q in range(8):
            ref = pieces[2 * part + q // 4]
            to_rows = aligned(place(index[0] // 16, part, q), block)
            full[to_rows, columns] = ref[q % 4 * block : (q % 4 + 1) * block, :]
    out[...] = contract(arranged.at[arranged.shape[0] // 2 :], full)


def product_kept(arranged, full, out):
    out[...] = contract(arranged.at[: arranged.shape[0] // 2], full)


def add_quarters(one, two, *outs):
    for k in range(4):
        outs[k][...] = total((one, two), slice(32 * k, 32 * k + 32)).astype(outs[k].dtype)


def add_shares(one, two, three, four, own, other):
    value = total((one, two, three, four), slice(None))
    own[...] = value[:16].astype(BF)
    other[...] = value[16:].astype(BF)


def weave(block, index, own, got, out):
    parity = index[0] // 16 % 2
    mine, theirs = own[...].astype(F32), got[...].astype(F32)
    even = jnp.where(parity == 0, mine, theirs)
    odd = jnp.where(parity == 0, theirs, mine)
    pieces = []
    for i in range(8):
        columns = slice(i * block, (i + 1) * block)
        pieces += [even[:, columns], odd[:, columns]]
    out[...] = jnp.concatenate(pieces, axis=1).astype(BF)


def join_quarters(*refs):
    for k in range(4):
        refs[4][16 * k : 16 * k + 16, :] = refs[k][...]


def place_rows(index, one, two, out):
    for at, owner in owners(index[0], -1):
        rows = at % 8 * 16
        out[aligned(owner, 16), :] = (one, two)[at // 8][rows : rows + 16, :]


def shape(*dims, dtype=BF):
    return jax.ShapeDtypeStruct(dims, dtype)


def call(kernel, out_shape, scalars, arrays, scratch=(), flops=0, limit=16):
    vmem = pl.BlockSpec(memory_space=pltpu.VMEM)
    smem = pl.BlockSpec(memory_space=pltpu.SMEM)
    return pl.pallas_call(
        kernel,
        out_shape=out_shape,
        in_specs=[smem] * len(scalars) + [vmem] * len(arrays),
        out_specs=jax.tree.map(lambda _: vmem, out_shape),
        scratch_shapes=[pltpu.VMEM(dims, BF) for dims in scratch],
        compiler_params=pltpu.CompilerParams(vmem_limit_bytes=limit * MB),
        cost_estimate=pl.CostEstimate(
            flops=flops, bytes_accessed=sum(a.size * 2 for a in arrays), transcendentals=0
        ),
    )(*scalars, *arrays)


def move(value, function):
    pairs = [(16 * d + t, 16 * d + function(d % 2, t)) for d in range(16) for t in range(16)]
    return lax.ppermute(value, ("dp", "tensor"), pairs)


def swap_first(value):
    return move(value, lambda core, t: t ^ (8, 1)[core])


def swap_second(value):
    return move(value, lambda core, t: t ^ (1, 8)[core])


def shift(value, quarters):
    return move(value, lambda core, t: t // 8 * 8 + (t + 2 * quarters) % 8)


def shards(hidden, out_grad, weight, first_moment, second_moment, next_hidden):
    block = first_moment.shape[0]
    tokens, units = hidden.shape
    features = out_grad.shape[1]
    cuts = (0, units // 3 * 2, units)
    sizes = [cuts[p + 1] - cuts[p] for p in range(PARTS)]
    index = lax.axis_index(("dp", "tensor")).reshape(1)
    product = tokens * units * features

    def parts(rows, dtype=BF):
        return tuple(shape(rows, size, dtype=dtype) for size in sizes)

    hidden_got = swap_cores(hidden)
    own, other = call(
        functools.partial(turn, block),
        (shape(features // 2, tokens), shape(features // 2, tokens)),
        [index],
        [out_grad],
        [(features, tokens)],
    )
    got = swap_cores(other)
    scratch = [(PARTS, 4 * block, 2 * tokens), (2 * tokens, units)]
    sent = call(
        functools.partial(grad_sent, cuts, block),
        parts(4 * block),
        [index],
        [own, got, hidden, hidden_got],
        scratch,
        flops=product,
    )
    arrived = [swap(sent[p], p, 0) for p in range(PARTS)]
    next_got = swap_cores(next_hidden)
    moments = shape(block, units, dtype=F32)
    input_grad, arranged, current, *kept = call(
        functools.partial(grad_kept, cuts, block),
        (shape(tokens, units), shape(2 * tokens, units), moments)
        + parts(4 * block),
        [index],
        [own, got, hidden, hidden_got, out_grad, weight, next_hidden, next_got],
        scratch + [(256, units)],
        flops=3 * product,
        limit=28,
    )

    def pairs(upper, lower):
        return [array for p in range(PARTS) for array in (upper[p], lower[p])]

    for step in (1, 2):
        rows = 4 * block >> step
        sums = call(
            functools.partial(add_parts, rows),
            parts(rows) + parts(rows, F32),
            [],
            pairs(kept, arrived),
        )
        arrived, kept = [swap(sums[p], p, step) for p in range(PARTS)], sums[PARTS:]
    *held, first_new, second_new, new_weight = call(
        functools.partial(adam, cuts),
        parts(block) + (moments, moments, shape(block, units)),
        [],
        [first_moment, second_moment, current] + pairs(kept, arrived),
    )

    for step in (2, 1, 0):
        arrived = [swap(held[p], p, step) for p in range(PARTS)]
        if step:
            held = call(join_parts, parts(8 * block >> step), [], pairs(held, arrived))

    wide = features // 2
    sent, full = call(
        functools.partial(product_sent, cuts, block),
        (shape(tokens, wide), shape(wide, units)),
        [index],
        [arranged] + pairs(held, arrived),
        flops=product,
    )
    arrived = swap_first(sent)
    kept = call(product_kept, shape(tokens, wide), [], [arranged, full], flops=product)
    rows = tokens // 2
    sent, kept = call(
        functools.partial(add_parts, rows),
        (shape(rows, wide), shape(rows, wide, dtype=F32)),
        [],
        [kept, arrived],
    )
    quarters = call(
        add_quarters,
        (shape(32, wide, dtype=F32),) + (shape(32, wide),) * 3,
        [],
        [kept, swap_second(sent)],
    )
    share, lacking = call(
        add_shares,
        (shape(16, wide), shape(16, wide)),
        [],
        [quarters[0]] + [shift(quarters[k], k) for k in (2, 1, 3)],
    )
    value = call(
        functools.partial(weave, block),
        shape(16, features),
        [index],
        [share, swap_cores(lacking)],
    )

    others = {k: shift(value, k) for k in (2, 1, 3)}
    out = call(join_quarters, shape(64, features), [], [value] + [others[k] for k in (1, 2, 3)])
    out, = call(join_parts, (shape(128, features),), [], [out, swap_second(out)])
    next_out = call(place_rows, shape(tokens, features), [index], [out, swap_first(out)])
    return (input_grad, first_new, second_new, new_weight, next_out)


def solution(mesh):
    placed = (
        P("dp", "tensor"),
        P("dp", None),
        P("tensor", None),
        P("dp", "tensor"),
        P("dp", "tensor"),
        P("dp", "tensor"),
    )
    return jax.shard_map(
        shards,
        mesh=mesh,
        in_specs=placed,
        out_specs=(
            P("dp", "tensor"),
            P("dp", "tensor"),
            P("dp", "tensor"),
            P("dp", "tensor"),
            P("dp", None),
        ),
        check_vma=False,
    )
```

```python
import functools

import jax
import jax.numpy as jnp
import numpy as np
from jax import lax
from jax.experimental import pallas as pl
from jax.experimental.pallas import tpu as pltpu
from jax.sharding import PartitionSpec as P

beta_first = 0.9
beta_second = 0.95
learn_rate = 0.001
weight_decay = 0.1
epsilon = 1e-08
correct_first = 0.999973438601112
correct_second = 0.99407947077967

BF = jnp.bfloat16
F32 = jnp.float32
MB = 1024 * 1024

GRAY = (0, 1, 3, 2)
CORE, X1, X2, Y = 1, 2, 4, 8
ENC = [(d % 2) | (GRAY[(d // 2) % 4] << 1) | ((d // 8) << 3) for d in range(16)]
DEC = [ENC.index(r) for r in range(16)]
SCATTER = (((Y, X2, X1), (X1, Y, X2)), ((X2, X1, Y), (X2, X1, Y)))
GATHER = (((X1, Y, X2), (Y, X2, X1)), ((X2, X1, Y), (X2, X1, Y)))
PARTS = 2


def flip(masks):
    return [(d, DEC[ENC[d] ^ masks[d % 2]]) for d in range(16)]


def relative(order, q):
    return (q >> 2 & 1) * order[0] | (q >> 1 & 1) * order[1] | (q & 1) * order[2]


def swap(value, orders, part, step):
    return lax.ppermute(value, "dp", flip([order[step] for order in orders[part]]))


def swap_cores(value):
    return lax.ppermute(value, "dp", flip((CORE, CORE)))


def aligned(index, size):
    return pl.ds(pl.multiple_of(index * size, size), size)


def place(device, orders, part, q):
    first, second = orders[part]
    move = jnp.where(device % 2 == 0, relative(first, q), relative(second, q)) // 2
    x = device // 2 % 4
    moved = ((x ^ (x // 2)) + device // 8 * 4) ^ move
    gray = moved % 4
    return moved - gray + (gray ^ (gray // 2))


def turn(block, index, out_grad, own, other, turned):
    turned[...] = out_grad[...].T
    parity = index[0] // 16 % 2
    for i in range(8):
        rows = slice(i * block, (i + 1) * block)
        own[rows, :] = turned[aligned(2 * i + parity, block), :]
        other[rows, :] = turned[aligned(2 * i + 1 - parity, block), :]


def grad_half(start, cuts, block, index, own, got, hidden, hidden_got, outs, lhs, rhs):
    tokens = hidden.shape[0]
    rhs[:tokens, :] = hidden[...]
    rhs[tokens:, :] = hidden_got[...]
    for part in range(PARTS):
        for q in range(4):
            rows = slice(q * block, (q + 1) * block)
            from_rows = aligned(place(index[0] // 16, SCATTER, part, start + q), block)
            lhs[part, rows, :tokens] = own[from_rows, :]
            lhs[part, rows, tokens:] = got[from_rows, :]
        outs[part][...] = jnp.dot(
            lhs[part], rhs[:, cuts[part] : cuts[part + 1]], preferred_element_type=F32
        ).astype(BF)


def grad_sent(cuts, block, index, own, got, hidden, hidden_got, *rest):
    grad_half(4, cuts, block, index, own, got, hidden, hidden_got, rest[:PARTS], *rest[PARTS:])


def grad_kept(
    cuts, block, index, own, got, hidden, hidden_got, out_grad, weight, nexts, nexts_got, *rest
):
    input_grad, rows_one, rows_two, current = rest[:4]
    rest, turned = rest[4:-1], rest[-1]
    grad_half(0, cuts, block, index, own, got, hidden, hidden_got, rest[:PARTS], *rest[PARTS:])
    input_grad[...] = contract(out_grad, weight)
    first = index[0] // 16 * block
    columns = pl.ds(pl.multiple_of(first // 128 * 128, 128), turned.shape[0])
    turned[...] = weight[:, columns].T
    current[...] = turned[pl.ds(pl.multiple_of(first % 128, 16), block), :].astype(F32)
    for place_one, place_two, owner in owners(index[0] % 16, 1):
        rows = aligned(owner, 16)
        for out, at in ((rows_one, place_one), (rows_two, place_two)):
            out[32 * at : 32 * at + 16, :] = nexts[rows, :]
            out[32 * at + 16 : 32 * at + 32, :] = nexts_got[rows, :]


def owners(tensor, sign):
    upper, low, quarter = tensor // 8, tensor % 2, tensor % 8 // 2
    for y in range(2):
        for b in range(2):
            for k in range(4):
                owner = (upper + y) % 2 * 8 + (quarter + sign * k + 4) % 4 * 2 + (low + b) % 2
                yield y * 8 + b * 4 + k, b * 8 + y * 4 + k, owner


def total(terms, rows):
    result = terms[0][rows, :].astype(F32)
    for term in terms[1:]:
        result = result + term[rows, :].astype(F32)
    return result


def add_parts(size, *refs):
    terms, outs = refs[: -2 * PARTS], refs[-2 * PARTS :]
    for part in range(PARTS):
        mine = terms[2 * part : 2 * part + 2]
        outs[part][...] = total(mine, slice(size, 2 * size)).astype(BF)
        outs[PARTS + part][...] = total(mine, slice(0, size))


def join_parts(*refs):
    for part in range(PARTS):
        upper, lower = refs[2 * part : 2 * part + 2]
        out = refs[2 * PARTS + part]
        rows = upper.shape[0]
        out[:rows, :] = upper[...]
        out[rows:, :] = lower[...]


def adam(cuts, first_moment, second_moment, current, *refs):
    terms, outs = refs[: 2 * PARTS], refs[2 * PARTS :]
    for part in range(PARTS):
        columns = slice(cuts[part], cuts[part + 1])
        grad = total(terms[2 * part : 2 * part + 2], slice(None))
        first_new = beta_first * first_moment[:, columns] + (1.0 - beta_first) * grad
        second_new = beta_second * second_moment[:, columns] + (1.0 - beta_second) * grad * grad
        update = first_new / correct_first / (jnp.sqrt(second_new / correct_second) + epsilon)
        old = current[:, columns]
        new_weight = (old - learn_rate * (update + weight_decay * old)).astype(BF)
        outs[part][...] = new_weight
        outs[PARTS][:, columns] = first_new
        outs[PARTS + 1][:, columns] = second_new
        outs[PARTS + 2][:, columns] = new_weight


def contract(one, two):
    return lax.dot_general(
        one[...], two[...], (((1,), (1,)), ((), ())), preferred_element_type=F32
    ).astype(BF)


def product_sent(cuts, block, cut, index, rows_one, rows_two, *rest):
    pieces, (out_one, out_two, full) = rest[: 2 * PARTS], rest[2 * PARTS :]
    for part in range(PARTS):
        columns = slice(cuts[part], cuts[part + 1])
        for q in range(8):
            ref = pieces[2 * part + q // 4]
            to_rows = aligned(place(index[0] // 16, GATHER, part, q), block)
            full[to_rows, columns] = ref[q % 4 * block : (q % 4 + 1) * block, :]
    half = rows_one.shape[0] // 2
    out_one[...] = contract(rows_one.at[half:], full.at[:cut])
    out_two[...] = contract(rows_two.at[half:], full.at[cut:])


def product_kept(cut, rows_one, rows_two, full, out_one, out_two):
    half = rows_one.shape[0] // 2
    out_one[...] = contract(rows_one.at[:half], full.at[:cut])
    out_two[...] = contract(rows_two.at[:half], full.at[cut:])


def add_quarters(cut, *refs):
    terms, outs = refs[: 2 * PARTS], refs[2 * PARTS :]
    for part, columns in enumerate((slice(0, cut), slice(cut, None))):
        for k in range(4):
            rows = total(terms[2 * part : 2 * part + 2], slice(32 * k, 32 * k + 32))
            outs[k][:, columns] = rows.astype(outs[k].dtype)


def add_shares(one, two, three, four, own, other):
    value = total((one, two, three, four), slice(None))
    own[...] = value[:16].astype(BF)
    other[...] = value[16:].astype(BF)


def weave(block, index, own, got, out):
    parity = index[0] // 16 % 2
    mine, theirs = own[...].astype(F32), got[...].astype(F32)
    even = jnp.where(parity == 0, mine, theirs)
    odd = jnp.where(parity == 0, theirs, mine)
    pieces = []
    for i in range(8):
        columns = slice(i * block, (i + 1) * block)
        pieces += [even[:, columns], odd[:, columns]]
    out[...] = jnp.concatenate(pieces, axis=1).astype(BF)


def join_quarters(cut, *refs):
    quarters, outs = refs[:4], refs[4:]
    for part, columns in enumerate((slice(0, cut), slice(cut, None))):
        for k in range(4):
            outs[part][16 * k : 16 * k + 16, :] = quarters[k][:, columns]


def place_rows(cut, index, one, one_got, two, two_got, out):
    for place_one, place_two, owner in owners(index[0] % 16, -1):
        rows = aligned(owner, 16)
        for place_in, refs, columns in (
            (place_one, (one, one_got), slice(0, cut)),
            (place_two, (two, two_got), slice(cut, None)),
        ):
            at = place_in % 8 * 16
            out[rows, columns] = refs[place_in // 8][at : at + 16, :]


def shape(*dims, dtype=BF):
    return jax.ShapeDtypeStruct(dims, dtype)


def call(kernel, out_shape, scalars, arrays, scratch=(), flops=0, limit=16):
    vmem = pl.BlockSpec(memory_space=pltpu.VMEM)
    smem = pl.BlockSpec(memory_space=pltpu.SMEM)
    return pl.pallas_call(
        kernel,
        out_shape=out_shape,
        in_specs=[smem] * len(scalars) + [vmem] * len(arrays),
        out_specs=jax.tree.map(lambda _: vmem, out_shape),
        scratch_shapes=[pltpu.VMEM(dims, BF) for dims in scratch],
        compiler_params=pltpu.CompilerParams(vmem_limit_bytes=limit * MB),
        cost_estimate=pl.CostEstimate(
            flops=flops, bytes_accessed=sum(a.size * 2 for a in arrays), transcendentals=0
        ),
    )(*scalars, *arrays)


def move(value, function):
    return lax.ppermute(value, "tensor", [(t, function(t)) for t in range(16)])


def swap_upper(value):
    return move(value, lambda t: (t + 8) % 16)


def swap_low(value):
    return move(value, lambda t: t ^ 1)


def shift(value, quarters):
    return move(value, lambda t: t // 8 * 8 + (t + 2 * quarters) % 8)


def shards(hidden, out_grad, weight, first_moment, second_moment, next_hidden):
    block = first_moment.shape[0]
    tokens, units = hidden.shape
    features = out_grad.shape[1]
    cuts = (0, units // 3 * 2, units)
    sizes = [cuts[p + 1] - cuts[p] for p in range(PARTS)]
    index = lax.axis_index(("dp", "tensor")).reshape(1)
    product = tokens * units * features

    def parts(rows, dtype=BF):
        return tuple(shape(rows, size, dtype=dtype) for size in sizes)

    hidden_got = swap_cores(hidden)
    own, other = call(
        functools.partial(turn, block),
        (shape(features // 2, tokens), shape(features // 2, tokens)),
        [index],
        [out_grad],
        [(features, tokens)],
    )
    got = swap_cores(other)
    scratch = [(PARTS, 4 * block, 2 * tokens), (2 * tokens, units)]
    sent = call(
        functools.partial(grad_sent, cuts, block),
        parts(4 * block),
        [index],
        [own, got, hidden, hidden_got],
        scratch,
        flops=product,
    )
    arrived = [swap(sent[p], SCATTER, p, 0) for p in range(PARTS)]
    next_got = swap_cores(next_hidden)
    moments = shape(block, units, dtype=F32)
    input_grad, rows_one, rows_two, current, *kept = call(
        functools.partial(grad_kept, cuts, block),
        (shape(tokens, units), shape(2 * tokens, units), shape(2 * tokens, units), moments)
        + parts(4 * block),
        [index],
        [own, got, hidden, hidden_got, out_grad, weight, next_hidden, next_got],
        scratch + [(256, units)],
        flops=3 * product,
        limit=28,
    )

    def pairs(upper, lower):
        return [array for p in range(PARTS) for array in (upper[p], lower[p])]

    for step in (1, 2):
        rows = 4 * block >> step
        sums = call(
            functools.partial(add_parts, rows),
            parts(rows) + parts(rows, F32),
            [],
            pairs(kept, arrived),
        )
        arrived, kept = [swap(sums[p], SCATTER, p, step) for p in range(PARTS)], sums[PARTS:]
    *held, first_new, second_new, new_weight = call(
        functools.partial(adam, cuts),
        parts(block) + (moments, moments, shape(block, units)),
        [],
        [first_moment, second_moment, current] + pairs(kept, arrived),
    )

    for step in (2, 1, 0):
        arrived = [swap(held[p], GATHER, p, step) for p in range(PARTS)]
        if step:
            held = call(join_parts, parts(8 * block >> step), [], pairs(held, arrived))

    wide = features // 2
    cut = wide // 9 * 5
    half = (shape(tokens, cut), shape(tokens, wide - cut))
    sent_one, sent_two, full = call(
        functools.partial(product_sent, cuts, block, cut),
        half + (shape(wide, units),),
        [index],
        [rows_one, rows_two] + pairs(held, arrived),
        flops=product,
    )
    arrived = [swap_upper(sent_one), swap_low(sent_two)]
    kept = call(
        functools.partial(product_kept, cut), half, [], [rows_one, rows_two, full], flops=product
    )
    rows = tokens // 2
    sums = call(
        functools.partial(add_parts, rows),
        tuple(shape(rows, w, dtype=d) for d in (BF, F32) for w in (cut, wide - cut)),
        [],
        pairs(kept, arrived),
    )
    arrived = [swap_low(sums[0]), swap_upper(sums[1])]
    quarters = call(
        functools.partial(add_quarters, cut),
        (shape(32, wide, dtype=F32),) + (shape(32, wide),) * 3,
        [],
        pairs(sums[2:], arrived),
    )
    share, lacking = call(
        add_shares,
        (shape(16, wide), shape(16, wide)),
        [],
        [quarters[0]] + [shift(quarters[k], k) for k in (2, 1, 3)],
    )
    value = call(
        functools.partial(weave, block),
        shape(16, features),
        [index],
        [share, swap_cores(lacking)],
    )

    cut = features // 9 * 5
    widths = (cut, features - cut)
    others = {k: shift(value, k) for k in (2, 1, 3)}
    one, two = call(
        functools.partial(join_quarters, cut),
        tuple(shape(64, w) for w in widths),
        [],
        [value] + [others[k] for k in (1, 2, 3)],
    )
    arrived = [swap_low(one), swap_upper(two)]
    one, two = call(
        join_parts, tuple(shape(128, w) for w in widths), [], pairs((one, two), arrived)
    )
    arrived = [swap_upper(one), swap_low(two)]
    next_out = call(
        functools.partial(place_rows, cut),
        shape(tokens, features),
        [index],
        pairs((one, two), arrived),
    )
    return (input_grad, first_new, second_new, new_weight, next_out)


def solution(mesh):
    placed = (
        P("dp", "tensor"),
        P("dp", None),
        P("tensor", None),
        P("dp", "tensor"),
        P("dp", "tensor"),
        P("dp", "tensor"),
    )
    return jax.shard_map(
        shards,
        mesh=mesh,
        in_specs=placed,
        out_specs=(
            P("dp", "tensor"),
            P("dp", "tensor"),
            P("dp", "tensor"),
            P("dp", "tensor"),
            P("dp", None),
        ),
        check_vma=False,
    )
```

```python
import functools

import jax
import jax.numpy as jnp
import numpy as np
from jax import lax
from jax.experimental import pallas as pl
from jax.experimental.pallas import tpu as pltpu
from jax.sharding import PartitionSpec as P

beta_first = 0.9
beta_second = 0.95
learn_rate = 0.001
weight_decay = 0.1
epsilon = 1e-08
correct_first = 0.999973438601112
correct_second = 0.99407947077967

BF = jnp.bfloat16
F32 = jnp.float32
MB = 1024 * 1024

GRAY = (0, 1, 3, 2)
CORE, X1, X2, Y = 1, 2, 4, 8
ENC = [(d % 2) | (GRAY[(d // 2) % 4] << 1) | ((d // 8) << 3) for d in range(16)]
DEC = [ENC.index(r) for r in range(16)]
SCATTER = (((Y, X2, X1), (X1, Y, X2)), ((X2, X1, Y), (X2, X1, Y)))
GATHER = (((Y, X2, X1), (X1, Y, X2)), ((X2, X1, Y), (X2, X1, Y)))
PARTS = 2


def flip(masks):
    return [(d, DEC[ENC[d] ^ masks[d % 2]]) for d in range(16)]


def relative(order, q):
    return (q >> 2 & 1) * order[0] | (q >> 1 & 1) * order[1] | (q & 1) * order[2]


def swap(value, orders, part, step):
    return lax.ppermute(value, "dp", flip([order[step] for order in orders[part]]))


def swap_cores(value):
    return lax.ppermute(value, "dp", flip((CORE, CORE)))


def aligned(index, size):
    return pl.ds(pl.multiple_of(index * size, size), size)


def place(device, orders, part, q):
    first, second = orders[part]
    move = jnp.where(device % 2 == 0, relative(first, q), relative(second, q)) // 2
    x = device // 2 % 4
    moved = ((x ^ (x // 2)) + device // 8 * 4) ^ move
    gray = moved % 4
    return moved - gray + (gray ^ (gray // 2))


def turn(block, index, out_grad, own, other, turned):
    turned[...] = out_grad[...].T
    parity = index[0] // 16 % 2
    for i in range(8):
        rows = slice(i * block, (i + 1) * block)
        own[rows, :] = turned[aligned(2 * i + parity, block), :]
        other[rows, :] = turned[aligned(2 * i + 1 - parity, block), :]


def grad_half(start, cuts, block, index, own, got, hidden, hidden_got, outs, lhs, rhs):
    tokens = hidden.shape[0]
    rhs[:tokens, :] = hidden[...]
    rhs[tokens:, :] = hidden_got[...]
    for part in range(PARTS):
        for q in range(4):
            rows = slice(q * block, (q + 1) * block)
            from_rows = aligned(place(index[0] // 16, SCATTER, part, start + q), block)
            lhs[part, rows, :tokens] = own[from_rows, :]
            lhs[part, rows, tokens:] = got[from_rows, :]
        outs[part][...] = jnp.dot(
            lhs[part], rhs[:, cuts[part] : cuts[part + 1]], preferred_element_type=F32
        ).astype(BF)


def grad_sent(cuts, block, index, own, got, hidden, hidden_got, *rest):
    grad_half(4, cuts, block, index, own, got, hidden, hidden_got, rest[:PARTS], *rest[PARTS:])


def grad_kept(
    cuts, block, index, own, got, hidden, hidden_got, out_grad, weight, nexts, nexts_got, *rest
):
    input_grad, rows_one, rows_two, current = rest[:4]
    rest, turned = rest[4:-1], rest[-1]
    grad_half(0, cuts, block, index, own, got, hidden, hidden_got, rest[:PARTS], *rest[PARTS:])
    input_grad[...] = contract(out_grad, weight)
    first = index[0] // 16 * block
    columns = pl.ds(pl.multiple_of(first // 128 * 128, 128), turned.shape[0])
    turned[...] = weight[:, columns].T
    current[...] = turned[pl.ds(pl.multiple_of(first % 128, 16), block), :].astype(F32)
    for place_one, place_two, owner in owners(index[0] % 16, 1):
        rows = aligned(owner, 16)
        for out, at in ((rows_one, place_one), (rows_two, place_two)):
            out[32 * at : 32 * at + 16, :] = nexts[rows, :]
            out[32 * at + 16 : 32 * at + 32, :] = nexts_got[rows, :]


def owners(tensor, sign):
    upper, low, quarter = tensor // 8, tensor % 2, tensor % 8 // 2
    for y in range(2):
        for b in range(2):
            for k in range(4):
                owner = (upper + y) % 2 * 8 + (quarter + sign * k + 4) % 4 * 2 + (low + b) % 2
                yield y * 8 + b * 4 + k, b * 8 + y * 4 + k, owner


def total(terms, rows):
    result = terms[0][rows, :].astype(F32)
    for term in terms[1:]:
        result = result + term[rows, :].astype(F32)
    return result


def add_parts(size, *refs):
    terms, outs = refs[: -2 * PARTS], refs[-2 * PARTS :]
    for part in range(PARTS):
        mine = terms[2 * part : 2 * part + 2]
        outs[part][...] = total(mine, slice(size, 2 * size)).astype(BF)
        outs[PARTS + part][...] = total(mine, slice(0, size))


def join_parts(*refs):
    for part in range(PARTS):
        upper, lower = refs[2 * part : 2 * part + 2]
        out = refs[2 * PARTS + part]
        rows = upper.shape[0]
        out[:rows, :] = upper[...]
        out[rows:, :] = lower[...]


def adam(cuts, stored, first_moment, second_moment, current, *refs):
    terms, outs = refs[: 2 * PARTS], refs[2 * PARTS :]
    for part in range(PARTS):
        columns = slice(cuts[part], cuts[part + 1])
        grad = total(terms[2 * part : 2 * part + 2], slice(None))
        first_new = beta_first * first_moment[:, columns] + (1.0 - beta_first) * grad
        second_new = beta_second * second_moment[:, columns] + (1.0 - beta_second) * grad * grad
        update = first_new / correct_first / (jnp.sqrt(second_new / correct_second) + epsilon)
        old = current[:, columns]
        new_weight = (old - learn_rate * (update + weight_decay * old)).astype(BF)
        if stored:
            outs[0][:, columns] = first_new
            outs[1][:, columns] = second_new
            outs[2][:, columns] = new_weight
        else:
            outs[part][...] = new_weight


def contract(one, two):
    return lax.dot_general(
        one[...], two[...], (((1,), (1,)), ((), ())), preferred_element_type=F32
    ).astype(BF)


def product_sent(cuts, block, cut, index, rows_one, rows_two, *rest):
    pieces, (out_one, out_two, full) = rest[: 2 * PARTS], rest[2 * PARTS :]
    for part in range(PARTS):
        columns = slice(cuts[part], cuts[part + 1])
        for q in range(8):
            ref = pieces[2 * part + q // 4]
            to_rows = aligned(place(index[0] // 16, GATHER, part, q), block)
            full[to_rows, columns] = ref[q % 4 * block : (q % 4 + 1) * block, :]
    half = rows_one.shape[0] // 2
    out_one[...] = contract(rows_one.at[half:], full.at[:cut])
    out_two[...] = contract(rows_two.at[half:], full.at[cut:])


def product_kept(cut, rows_one, rows_two, full, out_one, out_two):
    half = rows_one.shape[0] // 2
    out_one[...] = contract(rows_one.at[:half], full.at[:cut])
    out_two[...] = contract(rows_two.at[:half], full.at[cut:])


def add_quarters(cut, one, one_got, two, two_got, own, left, right, before, after):
    for terms, columns, far in (
        ((one, one_got), slice(0, cut), left),
        ((two, two_got), slice(cut, None), right),
    ):
        own[:, columns] = total(terms, slice(0, 32))
        before[:, columns] = total(terms, slice(32, 64))
        far[...] = total(terms, slice(64, 96)).astype(BF)
        after[:, columns] = total(terms, slice(96, 128))


def pass_on(cut, before, after, left, right, before_out, after_out):
    before_out[:, :cut] = (before[:, :cut] + left[...].astype(F32)).astype(BF)
    before_out[:, cut:] = before[:, cut:].astype(BF)
    after_out[:, :cut] = after[:, :cut].astype(BF)
    after_out[:, cut:] = (after[:, cut:] + right[...].astype(F32)).astype(BF)


def add_shares(one, two, three, own, other):
    value = total((one, two, three), slice(None))
    own[...] = value[:16].astype(BF)
    other[...] = value[16:].astype(BF)


def weave(block, index, own, got, out):
    parity = index[0] // 16 % 2
    mine, theirs = own[...].astype(F32), got[...].astype(F32)
    even = jnp.where(parity == 0, mine, theirs)
    odd = jnp.where(parity == 0, theirs, mine)
    pieces = []
    for i in range(8):
        columns = slice(i * block, (i + 1) * block)
        pieces += [even[:, columns], odd[:, columns]]
    out[...] = jnp.concatenate(pieces, axis=1).astype(BF)


def split_far(from_before, from_after, left, right):
    half = left.shape[1]
    left[...] = from_before[:, :half]
    right[...] = from_after[:, half:]


def join_quarters(cut, own, from_before, from_after, left, right, *outs):
    far = jnp.concatenate([left[...], right[...]], axis=1)
    for part, columns in enumerate((slice(0, cut), slice(cut, None))):
        outs[part][0:16, :] = own[:, columns]
        outs[part][16:32, :] = from_before[:, columns]
        outs[part][32:48, :] = far[:, columns]
        outs[part][48:64, :] = from_after[:, columns]


def place_rows(cut, index, one, one_got, two, two_got, out):
    for place_one, place_two, owner in owners(index[0] % 16, -1):
        rows = aligned(owner, 16)
        for place_in, refs, columns in (
            (place_one, (one, one_got), slice(0, cut)),
            (place_two, (two, two_got), slice(cut, None)),
        ):
            at = place_in % 8 * 16
            out[rows, columns] = refs[place_in // 8][at : at + 16, :]


def shape(*dims, dtype=BF):
    return jax.ShapeDtypeStruct(dims, dtype)


def call(kernel, out_shape, scalars, arrays, scratch=(), flops=0, limit=16):
    vmem = pl.BlockSpec(memory_space=pltpu.VMEM)
    smem = pl.BlockSpec(memory_space=pltpu.SMEM)
    return pl.pallas_call(
        kernel,
        out_shape=out_shape,
        in_specs=[smem] * len(scalars) + [vmem] * len(arrays),
        out_specs=jax.tree.map(lambda _: vmem, out_shape),
        scratch_shapes=[pltpu.VMEM(dims, BF) for dims in scratch],
        compiler_params=pltpu.CompilerParams(vmem_limit_bytes=limit * MB),
        cost_estimate=pl.CostEstimate(
            flops=flops, bytes_accessed=sum(a.size * 2 for a in arrays), transcendentals=0
        ),
    )(*scalars, *arrays)


def move(value, function):
    return lax.ppermute(value, "tensor", [(t, function(t)) for t in range(16)])


def swap_upper(value):
    return move(value, lambda t: (t + 8) % 16)


def swap_low(value):
    return move(value, lambda t: t ^ 1)


def shift(value, quarters):
    return move(value, lambda t: t // 8 * 8 + (t + 2 * quarters) % 8)


def shards(hidden, out_grad, weight, first_moment, second_moment, next_hidden):
    block = first_moment.shape[0]
    tokens, units = hidden.shape
    features = out_grad.shape[1]
    cuts = (0, units // 3 * 2, units)
    sizes = [cuts[p + 1] - cuts[p] for p in range(PARTS)]
    index = lax.axis_index(("dp", "tensor")).reshape(1)
    product = tokens * units * features

    def parts(rows, dtype=BF):
        return tuple(shape(rows, size, dtype=dtype) for size in sizes)

    hidden_got = swap_cores(hidden)
    own, other = call(
        functools.partial(turn, block),
        (shape(features // 2, tokens), shape(features // 2, tokens)),
        [index],
        [out_grad],
        [(features, tokens)],
    )
    got = swap_cores(other)
    scratch = [(PARTS, 4 * block, 2 * tokens), (2 * tokens, units)]
    sent = call(
        functools.partial(grad_sent, cuts, block),
        parts(4 * block),
        [index],
        [own, got, hidden, hidden_got],
        scratch,
        flops=product,
    )
    arrived = [swap(sent[p], SCATTER, p, 0) for p in range(PARTS)]
    next_got = swap_cores(next_hidden)
    moments = shape(block, units, dtype=F32)
    input_grad, rows_one, rows_two, current, *kept = call(
        functools.partial(grad_kept, cuts, block),
        (shape(tokens, units), shape(2 * tokens, units), shape(2 * tokens, units), moments)
        + parts(4 * block),
        [index],
        [own, got, hidden, hidden_got, out_grad, weight, next_hidden, next_got],
        scratch + [(256, units)],
        flops=3 * product,
        limit=28,
    )

    def pairs(upper, lower):
        return [array for p in range(PARTS) for array in (upper[p], lower[p])]

    for step in (1, 2):
        rows = 4 * block >> step
        sums = call(
            functools.partial(add_parts, rows),
            parts(rows) + parts(rows, F32),
            [],
            pairs(kept, arrived),
        )
        arrived, kept = [swap(sums[p], SCATTER, p, step) for p in range(PARTS)], sums[PARTS:]
    inputs = [first_moment, second_moment, current] + pairs(kept, arrived)
    held = call(functools.partial(adam, cuts, False), parts(block), [], inputs)
    first_new, second_new, new_weight = call(
        functools.partial(adam, cuts, True), (moments, moments, shape(block, units)), [], inputs
    )

    for step in (2, 1, 0):
        arrived = [swap(held[p], GATHER, p, step) for p in range(PARTS)]
        if step:
            held = call(join_parts, parts(8 * block >> step), [], pairs(held, arrived))

    wide = features // 2
    cut = wide // 9 * 5
    half = (shape(tokens, cut), shape(tokens, wide - cut))
    sent_one, sent_two, full = call(
        functools.partial(product_sent, cuts, block, cut),
        half + (shape(wide, units),),
        [index],
        [rows_one, rows_two] + pairs(held, arrived),
        flops=product,
    )
    arrived = [swap_upper(sent_one), swap_low(sent_two)]
    kept = call(
        functools.partial(product_kept, cut), half, [], [rows_one, rows_two, full], flops=product
    )
    rows = tokens // 2
    sums = call(
        functools.partial(add_parts, rows),
        tuple(shape(rows, w, dtype=d) for d in (BF, F32) for w in (cut, wide - cut)),
        [],
        pairs(kept, arrived),
    )
    arrived = [swap_low(sums[0]), swap_upper(sums[1])]
    own, left, right, before, after = call(
        functools.partial(add_quarters, cut),
        (
            shape(32, wide, dtype=F32),
            shape(32, cut),
            shape(32, wide - cut),
            shape(32, wide, dtype=F32),
            shape(32, wide, dtype=F32),
        ),
        [],
        pairs(sums[2:], arrived),
    )
    sent = call(
        functools.partial(pass_on, cut),
        (shape(32, wide), shape(32, wide)),
        [],
        [before, after, shift(left, 1), shift(right, -1)],
    )
    share, lacking = call(
        add_shares,
        (shape(16, wide), shape(16, wide)),
        [],
        [own, shift(sent[0], 1), shift(sent[1], -1)],
    )
    value = call(
        functools.partial(weave, block),
        shape(16, features),
        [index],
        [share, swap_cores(lacking)],
    )

    cut = features // 9 * 5
    widths = (cut, features - cut)
    near = [shift(value, 1), shift(value, -1)]
    left, right = call(split_far, (shape(16, wide), shape(16, wide)), [], near)
    one, two = call(
        functools.partial(join_quarters, cut),
        tuple(shape(64, w) for w in widths),
        [],
        [value] + near + [shift(left, 1), shift(right, -1)],
    )
    arrived = [swap_low(one), swap_upper(two)]
    one, two = call(
        join_parts, tuple(shape(128, w) for w in widths), [], pairs((one, two), arrived)
    )
    arrived = [swap_upper(one), swap_low(two)]
    next_out = call(
        functools.partial(place_rows, cut),
        shape(tokens, features),
        [index],
        pairs((one, two), arrived),
    )
    return (input_grad, first_new, second_new, new_weight, next_out)


def solution(mesh):
    placed = (
        P("dp", "tensor"),
        P("dp", None),
        P("tensor", None),
        P("dp", "tensor"),
        P("dp", "tensor"),
        P("dp", "tensor"),
    )
    return jax.shard_map(
        shards,
        mesh=mesh,
        in_specs=placed,
        out_specs=(
            P("dp", "tensor"),
            P("dp", "tensor"),
            P("dp", "tensor"),
            P("dp", "tensor"),
            P("dp", None),
        ),
        check_vma=False,
    )
```

```python
import functools

import jax
import jax.numpy as jnp
import numpy as np
from jax import lax
from jax.experimental import pallas as pl
from jax.experimental.pallas import tpu as pltpu
from jax.sharding import PartitionSpec as P

beta_first = 0.9
beta_second = 0.95
learn_rate = 0.001
weight_decay = 0.1
epsilon = 1e-08
correct_first = 0.999973438601112
correct_second = 0.99407947077967

BF = jnp.bfloat16
F32 = jnp.float32
MB = 1024 * 1024

GRAY = (0, 1, 3, 2)
CORE, X1, X2, Y = 1, 2, 4, 8
ENC = [(d % 2) | (GRAY[(d // 2) % 4] << 1) | ((d // 8) << 3) for d in range(16)]
DEC = [ENC.index(r) for r in range(16)]
SCATTER = (((X1, X2, Y), (X2, Y, X1)), ((Y, X1, X2), (Y, X1, X2)))
GATHER = (((X2, Y, X1), (X1, X2, Y)), ((Y, X1, X2), (Y, X1, X2)))
PARTS = 2


def flip(masks):
    return [(d, DEC[ENC[d] ^ masks[d % 2]]) for d in range(16)]


def relative(order, q):
    return (q >> 2 & 1) * order[0] | (q >> 1 & 1) * order[1] | (q & 1) * order[2]


def swap(value, orders, part, step):
    return lax.ppermute(value, "dp", flip([order[step] for order in orders[part]]))


def swap_cores(value):
    return lax.ppermute(value, "dp", flip((CORE, CORE)))


def aligned(index, size):
    return pl.ds(pl.multiple_of(index * size, size), size)


def place(device, orders, part, q):
    first, second = orders[part]
    move = jnp.where(device % 2 == 0, relative(first, q), relative(second, q)) // 2
    x = device // 2 % 4
    moved = ((x ^ (x // 2)) + device // 8 * 4) ^ move
    gray = moved % 4
    return moved - gray + (gray ^ (gray // 2))


def turn(block, index, out_grad, own, other, turned):
    turned[...] = out_grad[...].T
    parity = index[0] // 16 % 2
    for i in range(8):
        rows = slice(i * block, (i + 1) * block)
        own[rows, :] = turned[aligned(2 * i + parity, block), :]
        other[rows, :] = turned[aligned(2 * i + 1 - parity, block), :]


def grad_half(start, cuts, block, index, own, got, hidden, hidden_got, outs, lhs, rhs):
    tokens = hidden.shape[0]
    rhs[:tokens, :] = hidden[...]
    rhs[tokens:, :] = hidden_got[...]
    for part in range(PARTS):
        for q in range(4):
            rows = slice(q * block, (q + 1) * block)
            from_rows = aligned(place(index[0] // 16, SCATTER, part, start + q), block)
            lhs[part, rows, :tokens] = own[from_rows, :]
            lhs[part, rows, tokens:] = got[from_rows, :]
        outs[part][...] = jnp.dot(
            lhs[part], rhs[:, cuts[part] : cuts[part + 1]], preferred_element_type=F32
        ).astype(BF)


def grad_sent(cuts, block, index, own, got, hidden, hidden_got, *rest):
    grad_half(4, cuts, block, index, own, got, hidden, hidden_got, rest[:PARTS], *rest[PARTS:])


def grad_kept(
    cuts, block, index, own, got, hidden, hidden_got, out_grad, weight, nexts, nexts_got, *rest
):
    input_grad, rows_one, rows_two, current = rest[:4]
    rest, turned = rest[4:-1], rest[-1]
    grad_half(0, cuts, block, index, own, got, hidden, hidden_got, rest[:PARTS], *rest[PARTS:])
    input_grad[...] = contract(out_grad, weight)
    first = index[0] // 16 * block
    columns = pl.ds(pl.multiple_of(first // 128 * 128, 128), turned.shape[0])
    turned[...] = weight[:, columns].T
    current[...] = turned[pl.ds(pl.multiple_of(first % 128, 16), block), :].astype(F32)
    for place_one, place_two, owner in owners(index[0] % 16, 1):
        rows = aligned(owner, 16)
        for out, at in ((rows_one, place_one), (rows_two, place_two)):
            out[32 * at : 32 * at + 16, :] = nexts[rows, :]
            out[32 * at + 16 : 32 * at + 32, :] = nexts_got[rows, :]


def owners(tensor, sign):
    upper, low, quarter = tensor // 8, tensor % 2, tensor % 8 // 2
    for y in range(2):
        for b in range(2):
            for k in range(4):
                owner = (upper + y) % 2 * 8 + (quarter + sign * k + 4) % 4 * 2 + (low + b) % 2
                yield y * 8 + b * 4 + k, b * 8 + y * 4 + k, owner


def total(terms, rows):
    result = terms[0][rows, :].astype(F32)
    for term in terms[1:]:
        result = result + term[rows, :].astype(F32)
    return result


def add_parts(size, *refs):
    terms, outs = refs[: -2 * PARTS], refs[-2 * PARTS :]
    for part in range(PARTS):
        mine = terms[2 * part : 2 * part + 2]
        outs[part][...] = total(mine, slice(size, 2 * size)).astype(BF)
        outs[PARTS + part][...] = total(mine, slice(0, size))


def join_parts(*refs):
    for part in range(PARTS):
        upper, lower = refs[2 * part : 2 * part + 2]
        out = refs[2 * PARTS + part]
        rows = upper.shape[0]
        out[:rows, :] = upper[...]
        out[rows:, :] = lower[...]


def adam(cuts, stored, first_moment, second_moment, current, *refs):
    terms, outs = refs[: 2 * PARTS], refs[2 * PARTS :]
    for part in range(PARTS):
        columns = slice(cuts[part], cuts[part + 1])
        grad = total(terms[2 * part : 2 * part + 2], slice(None))
        first_new = beta_first * first_moment[:, columns] + (1.0 - beta_first) * grad
        second_new = beta_second * second_moment[:, columns] + (1.0 - beta_second) * grad * grad
        update = first_new / correct_first / (jnp.sqrt(second_new / correct_second) + epsilon)
        old = current[:, columns]
        new_weight = (old - learn_rate * (update + weight_decay * old)).astype(BF)
        if stored:
            outs[0][:, columns] = first_new
            outs[1][:, columns] = second_new
            outs[2][:, columns] = new_weight
        else:
            outs[part][...] = new_weight


def contract(one, two):
    return lax.dot_general(
        one[...], two[...], (((1,), (1,)), ((), ())), preferred_element_type=F32
    ).astype(BF)


def product_sent(cuts, block, cut, index, rows_one, rows_two, *rest):
    pieces, (out_one, out_two, full) = rest[: 2 * PARTS], rest[2 * PARTS :]
    for part in range(PARTS):
        columns = slice(cuts[part], cuts[part + 1])
        for q in range(8):
            ref = pieces[2 * part + q // 4]
            to_rows = aligned(place(index[0] // 16, GATHER, part, q), block)
            full[to_rows, columns] = ref[q % 4 * block : (q % 4 + 1) * block, :]
    half = rows_one.shape[0] // 2
    out_one[...] = contract(rows_one.at[half:], full.at[:cut])
    out_two[...] = contract(rows_two.at[half:], full.at[cut:])


def product_kept(cut, rows_one, rows_two, full, out_one, out_two):
    half = rows_one.shape[0] // 2
    out_one[...] = contract(rows_one.at[:half], full.at[:cut])
    out_two[...] = contract(rows_two.at[:half], full.at[cut:])


def add_quarters(cut, *refs):
    terms, outs = refs[: 2 * PARTS], refs[2 * PARTS :]
    for part, columns in enumerate((slice(0, cut), slice(cut, None))):
        for k in range(4):
            rows = total(terms[2 * part : 2 * part + 2], slice(32 * k, 32 * k + 32))
            outs[k][:, columns] = rows.astype(outs[k].dtype)


def add_shares(one, two, three, four, own, other):
    value = total((one, two, three, four), slice(None))
    own[...] = value[:16].astype(BF)
    other[...] = value[16:].astype(BF)


def weave(block, index, own, got, out):
    parity = index[0] // 16 % 2
    mine, theirs = own[...].astype(F32), got[...].astype(F32)
    even = jnp.where(parity == 0, mine, theirs)
    odd = jnp.where(parity == 0, theirs, mine)
    pieces = []
    for i in range(8):
        columns = slice(i * block, (i + 1) * block)
        pieces += [even[:, columns], odd[:, columns]]
    out[...] = jnp.concatenate(pieces, axis=1).astype(BF)


def join_quarters(cut, *refs):
    quarters, outs = refs[:4], refs[4:]
    for part, columns in enumerate((slice(0, cut), slice(cut, None))):
        for k in range(4):
            outs[part][16 * k : 16 * k + 16, :] = quarters[k][:, columns]


def place_rows(cut, index, one, one_got, two, two_got, out):
    for place_one, place_two, owner in owners(index[0] % 16, -1):
        rows = aligned(owner, 16)
        for place_in, refs, columns in (
            (place_one, (one, one_got), slice(0, cut)),
            (place_two, (two, two_got), slice(cut, None)),
        ):
            at = place_in % 8 * 16
            out[rows, columns] = refs[place_in // 8][at : at + 16, :]


def shape(*dims, dtype=BF):
    return jax.ShapeDtypeStruct(dims, dtype)


def call(kernel, out_shape, scalars, arrays, scratch=(), flops=0, limit=16):
    vmem = pl.BlockSpec(memory_space=pltpu.VMEM)
    smem = pl.BlockSpec(memory_space=pltpu.SMEM)
    return pl.pallas_call(
        kernel,
        out_shape=out_shape,
        in_specs=[smem] * len(scalars) + [vmem] * len(arrays),
        out_specs=jax.tree.map(lambda _: vmem, out_shape),
        scratch_shapes=[pltpu.VMEM(dims, BF) for dims in scratch],
        compiler_params=pltpu.CompilerParams(vmem_limit_bytes=limit * MB),
        cost_estimate=pl.CostEstimate(
            flops=flops, bytes_accessed=sum(a.size * 2 for a in arrays), transcendentals=0
        ),
    )(*scalars, *arrays)


def move(value, function):
    return lax.ppermute(value, "tensor", [(t, function(t)) for t in range(16)])


def swap_upper(value):
    return move(value, lambda t: (t + 8) % 16)


def swap_low(value):
    return move(value, lambda t: t ^ 1)


def shift(value, quarters):
    return move(value, lambda t: t // 8 * 8 + (t + 2 * quarters) % 8)


def shards(hidden, out_grad, weight, first_moment, second_moment, next_hidden):
    block = first_moment.shape[0]
    tokens, units = hidden.shape
    features = out_grad.shape[1]
    cuts = (0, units // 3 * 2, units)
    sizes = [cuts[p + 1] - cuts[p] for p in range(PARTS)]
    index = lax.axis_index(("dp", "tensor")).reshape(1)
    product = tokens * units * features

    def parts(rows, dtype=BF):
        return tuple(shape(rows, size, dtype=dtype) for size in sizes)

    hidden_got = swap_cores(hidden)
    own, other = call(
        functools.partial(turn, block),
        (shape(features // 2, tokens), shape(features // 2, tokens)),
        [index],
        [out_grad],
        [(features, tokens)],
    )
    got = swap_cores(other)
    scratch = [(PARTS, 4 * block, 2 * tokens), (2 * tokens, units)]
    sent = call(
        functools.partial(grad_sent, cuts, block),
        parts(4 * block),
        [index],
        [own, got, hidden, hidden_got],
        scratch,
        flops=product,
    )
    arrived = [swap(sent[p], SCATTER, p, 0) for p in range(PARTS)]
    next_got = swap_cores(next_hidden)
    moments = shape(block, units, dtype=F32)
    input_grad, rows_one, rows_two, current, *kept = call(
        functools.partial(grad_kept, cuts, block),
        (shape(tokens, units), shape(2 * tokens, units), shape(2 * tokens, units), moments)
        + parts(4 * block),
        [index],
        [own, got, hidden, hidden_got, out_grad, weight, next_hidden, next_got],
        scratch + [(256, units)],
        flops=3 * product,
        limit=28,
    )

    def pairs(upper, lower):
        return [array for p in range(PARTS) for array in (upper[p], lower[p])]

    for step in (1, 2):
        rows = 4 * block >> step
        sums = call(
            functools.partial(add_parts, rows),
            parts(rows) + parts(rows, F32),
            [],
            pairs(kept, arrived),
        )
        arrived, kept = [swap(sums[p], SCATTER, p, step) for p in range(PARTS)], sums[PARTS:]
    inputs = [first_moment, second_moment, current] + pairs(kept, arrived)
    held = call(functools.partial(adam, cuts, False), parts(block), [], inputs)
    first_new, second_new, new_weight = call(
        functools.partial(adam, cuts, True), (moments, moments, shape(block, units)), [], inputs
    )

    for step in (2, 1, 0):
        arrived = [swap(held[p], GATHER, p, step) for p in range(PARTS)]
        if step:
            held = call(join_parts, parts(8 * block >> step), [], pairs(held, arrived))

    wide = features // 2
    cut = wide // 9 * 5
    half = (shape(tokens, cut), shape(tokens, wide - cut))
    sent_one, sent_two, full = call(
        functools.partial(product_sent, cuts, block, cut),
        half + (shape(wide, units),),
        [index],
        [rows_one, rows_two] + pairs(held, arrived),
        flops=product,
    )
    arrived = [swap_upper(sent_one), swap_low(sent_two)]
    kept = call(
        functools.partial(product_kept, cut), half, [], [rows_one, rows_two, full], flops=product
    )
    rows = tokens // 2
    sums = call(
        functools.partial(add_parts, rows),
        tuple(shape(rows, w, dtype=d) for d in (BF, F32) for w in (cut, wide - cut)),
        [],
        pairs(kept, arrived),
    )
    arrived = [swap_low(sums[0]), swap_upper(sums[1])]
    quarters = call(
        functools.partial(add_quarters, cut),
        (shape(32, wide, dtype=F32),) + (shape(32, wide),) * 3,
        [],
        pairs(sums[2:], arrived),
    )
    share, lacking = call(
        add_shares,
        (shape(16, wide), shape(16, wide)),
        [],
        [quarters[0]] + [shift(quarters[k], k) for k in (2, 1, 3)],
    )
    value = call(
        functools.partial(weave, block),
        shape(16, features),
        [index],
        [share, swap_cores(lacking)],
    )

    cut = features // 9 * 5
    widths = (cut, features - cut)
    others = {k: shift(value, k) for k in (2, 1, 3)}
    one, two = call(
        functools.partial(join_quarters, cut),
        tuple(shape(64, w) for w in widths),
        [],
        [value] + [others[k] for k in (1, 2, 3)],
    )
    arrived = [swap_low(one), swap_upper(two)]
    one, two = call(
        join_parts, tuple(shape(128, w) for w in widths), [], pairs((one, two), arrived)
    )
    arrived = [swap_upper(one), swap_low(two)]
    next_out = call(
        functools.partial(place_rows, cut),
        shape(tokens, features),
        [index],
        pairs((one, two), arrived),
    )
    return (input_grad, first_new, second_new, new_weight, next_out)


def solution(mesh):
    placed = (
        P("dp", "tensor"),
        P("dp", None),
        P("tensor", None),
        P("dp", "tensor"),
        P("dp", "tensor"),
        P("dp", "tensor"),
    )
    return jax.shard_map(
        shards,
        mesh=mesh,
        in_specs=placed,
        out_specs=(
            P("dp", "tensor"),
            P("dp", "tensor"),
            P("dp", "tensor"),
            P("dp", "tensor"),
            P("dp", None),
        ),
        check_vma=False,
    )
```

```python
import functools

import jax
import jax.numpy as jnp
import numpy as np
from jax import lax
from jax.experimental import pallas as pl
from jax.experimental.pallas import tpu as pltpu
from jax.sharding import PartitionSpec as P

beta_first = 0.9
beta_second = 0.95
learn_rate = 0.001
weight_decay = 0.1
epsilon = 1e-08
correct_first = 0.999973438601112
correct_second = 0.99407947077967

BF = jnp.bfloat16
F32 = jnp.float32
MB = 1024 * 1024

GRAY = (0, 1, 3, 2)
CORE, X1, X2, Y = 1, 2, 4, 8
ENC = [(d % 2) | (GRAY[(d // 2) % 4] << 1) | ((d // 8) << 3) for d in range(16)]
DEC = [ENC.index(r) for r in range(16)]
SCATTER = (((X1, X2, Y), (X2, Y, X1)), ((Y, X1, X2), (Y, X1, X2)))
GATHER = (((X2, Y, X1), (X1, X2, Y)), ((Y, X1, X2), (Y, X1, X2)))
PARTS = 2


def flip(masks):
    return [(d, DEC[ENC[d] ^ masks[d % 2]]) for d in range(16)]


def relative(order, q):
    return (q >> 2 & 1) * order[0] | (q >> 1 & 1) * order[1] | (q & 1) * order[2]


def swap(value, orders, part, step):
    return lax.ppermute(value, "dp", flip([order[step] for order in orders[part]]))


def swap_cores(value):
    return lax.ppermute(value, "dp", flip((CORE, CORE)))


def aligned(index, size):
    return pl.ds(pl.multiple_of(index * size, size), size)


def place(device, orders, part, q):
    first, second = orders[part]
    move = jnp.where(device % 2 == 0, relative(first, q), relative(second, q)) // 2
    x = device // 2 % 4
    moved = ((x ^ (x // 2)) + device // 8 * 4) ^ move
    gray = moved % 4
    return moved - gray + (gray ^ (gray // 2))


def turn(block, index, out_grad, own, other, turned):
    turned[...] = out_grad[...].T
    parity = index[0] // 16 % 2
    for i in range(8):
        rows = slice(i * block, (i + 1) * block)
        own[rows, :] = turned[aligned(2 * i + parity, block), :]
        other[rows, :] = turned[aligned(2 * i + 1 - parity, block), :]


def grad_half(start, cuts, block, index, own, got, hidden, hidden_got, outs, lhs, rhs):
    tokens = hidden.shape[0]
    rhs[:tokens, :] = hidden[...]
    rhs[tokens:, :] = hidden_got[...]
    for part in range(PARTS):
        for q in range(4):
            rows = slice(q * block, (q + 1) * block)
            from_rows = aligned(place(index[0] // 16, SCATTER, part, start + q), block)
            lhs[part, rows, :tokens] = own[from_rows, :]
            lhs[part, rows, tokens:] = got[from_rows, :]
        outs[part][...] = jnp.dot(
            lhs[part], rhs[:, cuts[part] : cuts[part + 1]], preferred_element_type=F32
        ).astype(BF)


def grad_sent(cuts, block, index, own, got, hidden, hidden_got, *rest):
    grad_half(4, cuts, block, index, own, got, hidden, hidden_got, rest[:PARTS], *rest[PARTS:])


def grad_kept(
    cuts, block, index, own, got, hidden, hidden_got, out_grad, weight, nexts, nexts_got, *rest
):
    input_grad, arranged, current = rest[:3]
    rest, turned = rest[3:-1], rest[-1]
    grad_half(0, cuts, block, index, own, got, hidden, hidden_got, rest[:PARTS], *rest[PARTS:])
    input_grad[...] = contract(out_grad, weight)
    first = index[0] // 16 * block
    columns = pl.ds(pl.multiple_of(first // 128 * 128, 128), turned.shape[0])
    turned[...] = weight[:, columns].T
    current[...] = turned[pl.ds(pl.multiple_of(first % 128, 16), block), :].astype(F32)
    for at, owner in enumerate(owners(index[0] % 16, 1)):
        rows = aligned(owner, 16)
        arranged[32 * at : 32 * at + 16, :] = nexts[rows, :]
        arranged[32 * at + 16 : 32 * at + 32, :] = nexts_got[rows, :]


def owners(tensor, sign):
    upper, low, quarter = tensor // 8, tensor % 2, tensor % 8 // 2
    for y in range(2):
        for b in range(2):
            for k in range(4):
                yield (upper + y) % 2 * 8 + (quarter + sign * k + 4) % 4 * 2 + (low + b) % 2


def total(terms, rows):
    result = terms[0][rows, :].astype(F32)
    for term in terms[1:]:
        result = result + term[rows, :].astype(F32)
    return result


def add_parts(size, *refs):
    terms, outs = refs[: -2 * PARTS], refs[-2 * PARTS :]
    for part in range(PARTS):
        mine = terms[2 * part : 2 * part + 2]
        outs[part][...] = total(mine, slice(size, 2 * size)).astype(BF)
        outs[PARTS + part][...] = total(mine, slice(0, size))


def join_parts(*refs):
    for part in range(PARTS):
        upper, lower = refs[2 * part : 2 * part + 2]
        out = refs[2 * PARTS + part]
        rows = upper.shape[0]
        out[:rows, :] = upper[...]
        out[rows:, :] = lower[...]


def adam(cuts, stored, first_moment, second_moment, current, *refs):
    terms, outs = refs[: 2 * PARTS], refs[2 * PARTS :]
    for part in range(PARTS):
        columns = slice(cuts[part], cuts[part + 1])
        grad = total(terms[2 * part : 2 * part + 2], slice(None))
        first_new = beta_first * first_moment[:, columns] + (1.0 - beta_first) * grad
        second_new = beta_second * second_moment[:, columns] + (1.0 - beta_second) * grad * grad
        update = first_new / correct_first / (jnp.sqrt(second_new / correct_second) + epsilon)
        old = current[:, columns]
        new_weight = (old - learn_rate * (update + weight_decay * old)).astype(BF)
        if stored:
            outs[0][:, columns] = first_new
            outs[1][:, columns] = second_new
            outs[2][:, columns] = new_weight
        else:
            start = 0
            for out in outs:
                end = start + out.shape[1]
                low, high = max(start, cuts[part]), min(end, cuts[part + 1])
                if low < high:
                    piece = new_weight[:, low - cuts[part] : high - cuts[part]]
                    out[:, low - start : high - start] = piece
                start = end


def contract(one, two):
    return lax.dot_general(
        one[...], two[...], (((1,), (1,)), ((), ())), preferred_element_type=F32
    ).astype(BF)


def product_sent(cuts, block, index, arranged, *rest):
    pieces, outs, full = rest[: 2 * PARTS], rest[2 * PARTS : -1], rest[-1]
    for part in range(PARTS):
        columns = slice(cuts[part], cuts[part + 1])
        for q in range(8):
            ref = pieces[2 * part + q // 4]
            to_rows = aligned(place(index[0] // 16, GATHER, part, q), block)
            full[to_rows, columns] = ref[q % 4 * block : (q % 4 + 1) * block, :]
    rows = outs[0].shape[0]
    value = contract(arranged.at[rows:], full)
    for k, out in enumerate(outs):
        out[...] = value[k * rows : (k + 1) * rows]


def product_kept(arranged, full, out):
    out[...] = lax.dot_general(
        arranged[: out.shape[0], :],
        full[...],
        (((1,), (1,)), ((), ())),
        preferred_element_type=F32,
    )


def add_quarters(*refs):
    terms, outs = refs[:4], refs[4:]
    for k in range(4):
        outs[k][...] = total(terms, slice(32 * k, 32 * k + 32)).astype(outs[k].dtype)


def add_shares(one, two, three, four, own, other):
    value = total((one, two, three, four), slice(None))
    own[...] = value[:16].astype(BF)
    other[...] = value[16:].astype(BF)


def weave(block, index, own, got, out):
    parity = index[0] // 16 % 2
    mine, theirs = own[...].astype(F32), got[...].astype(F32)
    even = jnp.where(parity == 0, mine, theirs)
    odd = jnp.where(parity == 0, theirs, mine)
    pieces = []
    for i in range(8):
        columns = slice(i * block, (i + 1) * block)
        pieces += [even[:, columns], odd[:, columns]]
    out[...] = jnp.concatenate(pieces, axis=1).astype(BF)


def join_quarters(*refs):
    for k in range(4):
        refs[4][16 * k : 16 * k + 16, :] = refs[k][...]


def place_rows(index, *refs):
    for at, owner in enumerate(owners(index[0] % 16, -1)):
        rows = at % 4 * 16
        refs[4][aligned(owner, 16), :] = refs[at // 4][rows : rows + 16, :]


def shape(*dims, dtype=BF):
    return jax.ShapeDtypeStruct(dims, dtype)


def call(kernel, out_shape, scalars, arrays, scratch=(), flops=0, limit=16):
    vmem = pl.BlockSpec(memory_space=pltpu.VMEM)
    smem = pl.BlockSpec(memory_space=pltpu.SMEM)
    return pl.pallas_call(
        kernel,
        out_shape=out_shape,
        in_specs=[smem] * len(scalars) + [vmem] * len(arrays),
        out_specs=jax.tree.map(lambda _: vmem, out_shape),
        scratch_shapes=[pltpu.VMEM(dims, BF) for dims in scratch],
        compiler_params=pltpu.CompilerParams(vmem_limit_bytes=limit * MB),
        cost_estimate=pl.CostEstimate(
            flops=flops, bytes_accessed=sum(a.size * 2 for a in arrays), transcendentals=0
        ),
    )(*scalars, *arrays)


def move(value, function):
    return lax.ppermute(value, "tensor", [(t, function(t)) for t in range(16)])


def send_four(values):
    masks = (1, 8, 9)
    got = {m: move(v, lambda t, m=m: t ^ m) for m, v in reversed(list(zip(masks, values)))}
    return [got[m] for m in masks]


def shift(value, quarters):
    return move(value, lambda t: t // 8 * 8 + (t + 2 * quarters) % 8)


def shards(hidden, out_grad, weight, first_moment, second_moment, next_hidden):
    block = first_moment.shape[0]
    tokens, units = hidden.shape
    features = out_grad.shape[1]
    cuts = (0, units // 3 * 2, units)
    sizes = [cuts[p + 1] - cuts[p] for p in range(PARTS)]
    index = lax.axis_index(("dp", "tensor")).reshape(1)
    product = tokens * units * features
    gather_cuts = (0, units // 9 * 5, units)

    def parts(rows, dtype=BF):
        return tuple(shape(rows, size, dtype=dtype) for size in sizes)

    def gather_parts(rows):
        return tuple(shape(rows, gather_cuts[p + 1] - gather_cuts[p]) for p in range(PARTS))

    hidden_got = swap_cores(hidden)
    own, other = call(
        functools.partial(turn, block),
        (shape(features // 2, tokens), shape(features // 2, tokens)),
        [index],
        [out_grad],
        [(features, tokens)],
    )
    got = swap_cores(other)
    scratch = [(PARTS, 4 * block, 2 * tokens), (2 * tokens, units)]
    sent = call(
        functools.partial(grad_sent, cuts, block),
        parts(4 * block),
        [index],
        [own, got, hidden, hidden_got],
        scratch,
        flops=product,
    )
    arrived = [swap(sent[p], SCATTER, p, 0) for p in range(PARTS)]
    next_got = swap_cores(next_hidden)
    moments = shape(block, units, dtype=F32)
    input_grad, arranged, current, *kept = call(
        functools.partial(grad_kept, cuts, block),
        (shape(tokens, units), shape(2 * tokens, units), moments)
        + parts(4 * block),
        [index],
        [own, got, hidden, hidden_got, out_grad, weight, next_hidden, next_got],
        scratch + [(256, units)],
        flops=3 * product,
        limit=28,
    )

    def pairs(upper, lower):
        return [array for p in range(PARTS) for array in (upper[p], lower[p])]

    for step in (1, 2):
        rows = 4 * block >> step
        sums = call(
            functools.partial(add_parts, rows),
            parts(rows) + parts(rows, F32),
            [],
            pairs(kept, arrived),
        )
        arrived, kept = [swap(sums[p], SCATTER, p, step) for p in range(PARTS)], sums[PARTS:]
    inputs = [first_moment, second_moment, current] + pairs(kept, arrived)
    held = call(functools.partial(adam, cuts, False), gather_parts(block), [], inputs)
    first_new, second_new, new_weight = call(
        functools.partial(adam, cuts, True), (moments, moments, shape(block, units)), [], inputs
    )

    for step in (2, 1, 0):
        arrived = [swap(held[p], GATHER, p, step) for p in range(PARTS)]
        if step:
            held = call(join_parts, gather_parts(8 * block >> step), [], pairs(held, arrived))

    wide = features // 2
    rows = tokens // 2
    *sent, full = call(
        functools.partial(product_sent, gather_cuts, block),
        (shape(rows, wide),) * 3 + (shape(wide, units),),
        [index],
        [arranged] + pairs(held, arrived),
        flops=product * 3 // 2,
    )
    arrived = send_four(sent)
    kept = call(
        product_kept, shape(rows, wide, dtype=F32), [], [arranged, full], flops=product // 2
    )
    quarters = call(
        add_quarters,
        (shape(32, wide, dtype=F32),) + (shape(32, wide),) * 3,
        [],
        [kept] + arrived,
    )
    share, lacking = call(
        add_shares,
        (shape(16, wide), shape(16, wide)),
        [],
        [quarters[0]] + [shift(quarters[k], k) for k in (2, 1, 3)],
    )
    value = call(
        functools.partial(weave, block),
        shape(16, features),
        [index],
        [share, swap_cores(lacking)],
    )

    others = {k: shift(value, k) for k in (2, 1, 3)}
    out = call(join_quarters, shape(64, features), [], [value] + [others[k] for k in (1, 2, 3)])
    next_out = call(place_rows, shape(tokens, features), [index], [out] + send_four([out] * 3))
    return (input_grad, first_new, second_new, new_weight, next_out)


def solution(mesh):
    placed = (
        P("dp", "tensor"),
        P("dp", None),
        P("tensor", None),
        P("dp", "tensor"),
        P("dp", "tensor"),
        P("dp", "tensor"),
    )
    return jax.shard_map(
        shards,
        mesh=mesh,
        in_specs=placed,
        out_specs=(
            P("dp", "tensor"),
            P("dp", "tensor"),
            P("dp", "tensor"),
            P("dp", "tensor"),
            P("dp", None),
        ),
        check_vma=False,
    )
```

```python
import functools

import jax
import jax.numpy as jnp
import numpy as np
from jax import lax
from jax.experimental import pallas as pl
from jax.experimental.pallas import tpu as pltpu
from jax.sharding import PartitionSpec as P

beta_first = 0.9
beta_second = 0.95
learn_rate = 0.001
weight_decay = 0.1
epsilon = 1e-08
correct_first = 0.999973438601112
correct_second = 0.99407947077967

BF = jnp.bfloat16
F32 = jnp.float32
MB = 1024 * 1024

GRAY = (0, 1, 3, 2)
CORE, X1, X2, Y = 1, 2, 4, 8
ENC = [(d % 2) | (GRAY[(d // 2) % 4] << 1) | ((d // 8) << 3) for d in range(16)]
DEC = [ENC.index(r) for r in range(16)]
SCATTER = (((X1, X2, Y), (X2, Y, X1)), ((Y, X1, X2), (Y, X1, X2)))
GATHER = (((X2, Y, X1), (X1, X2, Y)), ((Y, X1, X2), (Y, X1, X2)))
PARTS = 2


def flip(masks):
    return [(d, DEC[ENC[d] ^ masks[d % 2]]) for d in range(16)]


def relative(order, q):
    return (q >> 2 & 1) * order[0] | (q >> 1 & 1) * order[1] | (q & 1) * order[2]


def swap(value, orders, part, step):
    return lax.ppermute(value, "dp", flip([order[step] for order in orders[part]]))


def swap_cores(value):
    return lax.ppermute(value, "dp", flip((CORE, CORE)))


def aligned(index, size):
    return pl.ds(pl.multiple_of(index * size, size), size)


def place(device, orders, part, q):
    first, second = orders[part]
    move = jnp.where(device % 2 == 0, relative(first, q), relative(second, q)) // 2
    x = device // 2 % 4
    moved = ((x ^ (x // 2)) + device // 8 * 4) ^ move
    gray = moved % 4
    return moved - gray + (gray ^ (gray // 2))


def turn(block, index, out_grad, own, other, turned):
    turned[...] = out_grad[...].T
    parity = index[0] // 16 % 2
    for i in range(8):
        rows = slice(i * block, (i + 1) * block)
        own[rows, :] = turned[aligned(2 * i + parity, block), :]
        other[rows, :] = turned[aligned(2 * i + 1 - parity, block), :]


def grad_half(start, cuts, block, index, own, got, hidden, hidden_got, outs, lhs, rhs):
    tokens = hidden.shape[0]
    rhs[:tokens, :] = hidden[...]
    rhs[tokens:, :] = hidden_got[...]
    for part in range(PARTS):
        for q in range(4):
            rows = slice(q * block, (q + 1) * block)
            from_rows = aligned(place(index[0] // 16, SCATTER, part, start + q), block)
            lhs[part, rows, :tokens] = own[from_rows, :]
            lhs[part, rows, tokens:] = got[from_rows, :]
        outs[part][...] = jnp.dot(
            lhs[part], rhs[:, cuts[part] : cuts[part + 1]], preferred_element_type=F32
        ).astype(BF)


def grad_sent(cuts, block, index, own, got, hidden, hidden_got, *rest):
    grad_half(4, cuts, block, index, own, got, hidden, hidden_got, rest[:PARTS], *rest[PARTS:])


def grad_kept(
    cuts, block, index, own, got, hidden, hidden_got, out_grad, weight, nexts, nexts_got, *rest
):
    input_grad, arranged, current = rest[:3]
    rest, turned = rest[3:-1], rest[-1]
    grad_half(0, cuts, block, index, own, got, hidden, hidden_got, rest[:PARTS], *rest[PARTS:])
    input_grad[...] = contract(out_grad, weight)
    first = index[0] // 16 * block
    columns = pl.ds(pl.multiple_of(first // 128 * 128, 128), turned.shape[0])
    turned[...] = weight[:, columns].T
    current[...] = turned[pl.ds(pl.multiple_of(first % 128, 16), block), :].astype(F32)
    for at, owner in enumerate(owners(index[0] % 16, 1)):
        rows = aligned(owner, 16)
        arranged[32 * at : 32 * at + 16, :] = nexts[rows, :]
        arranged[32 * at + 16 : 32 * at + 32, :] = nexts_got[rows, :]


def owners(tensor, sign):
    upper, low, quarter = tensor // 8, tensor % 2, tensor % 8 // 2
    for y in range(2):
        for b in range(2):
            for k in range(4):
                yield (upper + y) % 2 * 8 + (quarter + sign * k + 4) % 4 * 2 + (low + b) % 2


def total(terms, rows):
    result = terms[0][rows, :].astype(F32)
    for term in terms[1:]:
        result = result + term[rows, :].astype(F32)
    return result


def add_parts(size, *refs):
    terms, outs = refs[: -2 * PARTS], refs[-2 * PARTS :]
    for part in range(PARTS):
        mine = terms[2 * part : 2 * part + 2]
        outs[part][...] = total(mine, slice(size, 2 * size)).astype(BF)
        outs[PARTS + part][...] = total(mine, slice(0, size))


def join_parts(*refs):
    for part in range(PARTS):
        upper, lower = refs[2 * part : 2 * part + 2]
        out = refs[2 * PARTS + part]
        rows = upper.shape[0]
        out[:rows, :] = upper[...]
        out[rows:, :] = lower[...]


def adam(cuts, stored, first_moment, second_moment, current, *refs):
    terms, outs = refs[: 2 * PARTS], refs[2 * PARTS :]
    for part in range(PARTS):
        columns = slice(cuts[part], cuts[part + 1])
        grad = total(terms[2 * part : 2 * part + 2], slice(None))
        first_new = beta_first * first_moment[:, columns] + (1.0 - beta_first) * grad
        second_new = beta_second * second_moment[:, columns] + (1.0 - beta_second) * grad * grad
        update = first_new / correct_first / (jnp.sqrt(second_new / correct_second) + epsilon)
        old = current[:, columns]
        new_weight = (old - learn_rate * (update + weight_decay * old)).astype(BF)
        if stored:
            outs[0][:, columns] = first_new
            outs[1][:, columns] = second_new
            outs[2][:, columns] = new_weight
        else:
            outs[part][...] = new_weight


def contract(one, two):
    return lax.dot_general(
        one[...], two[...], (((1,), (1,)), ((), ())), preferred_element_type=F32
    ).astype(BF)


def product_sent(cuts, block, index, arranged, *rest):
    pieces, outs, full = rest[: 2 * PARTS], rest[2 * PARTS : -1], rest[-1]
    for part in range(PARTS):
        columns = slice(cuts[part], cuts[part + 1])
        for q in range(8):
            ref = pieces[2 * part + q // 4]
            to_rows = aligned(place(index[0] // 16, GATHER, part, q), block)
            full[to_rows, columns] = ref[q % 4 * block : (q % 4 + 1) * block, :]
    rows = outs[0].shape[0]
    value = contract(arranged.at[rows:], full)
    for k, out in enumerate(outs):
        out[...] = value[k * rows : (k + 1) * rows]


def product_kept(arranged, full, out):
    out[...] = lax.dot_general(
        arranged[: out.shape[0], :],
        full[...],
        (((1,), (1,)), ((), ())),
        preferred_element_type=F32,
    )


def add_quarters(*refs):
    terms, outs = refs[:4], refs[4:]
    for k in range(4):
        outs[k][...] = total(terms, slice(32 * k, 32 * k + 32)).astype(outs[k].dtype)


def add_shares(one, two, three, four, own, other):
    value = total((one, two, three, four), slice(None))
    own[...] = value[:16].astype(BF)
    other[...] = value[16:].astype(BF)


def weave(block, index, own, got, out):
    parity = index[0] // 16 % 2
    mine, theirs = own[...].astype(F32), got[...].astype(F32)
    even = jnp.where(parity == 0, mine, theirs)
    odd = jnp.where(parity == 0, theirs, mine)
    pieces = []
    for i in range(8):
        columns = slice(i * block, (i + 1) * block)
        pieces += [even[:, columns], odd[:, columns]]
    out[...] = jnp.concatenate(pieces, axis=1).astype(BF)


def join_quarters(*refs):
    for k in range(4):
        refs[4][16 * k : 16 * k + 16, :] = refs[k][...]


def place_rows(index, *refs):
    for at, owner in enumerate(owners(index[0] % 16, -1)):
        rows = at % 4 * 16
        refs[4][aligned(owner, 16), :] = refs[at // 4][rows : rows + 16, :]


def shape(*dims, dtype=BF):
    return jax.ShapeDtypeStruct(dims, dtype)


def call(kernel, out_shape, scalars, arrays, scratch=(), flops=0, limit=16):
    vmem = pl.BlockSpec(memory_space=pltpu.VMEM)
    smem = pl.BlockSpec(memory_space=pltpu.SMEM)
    return pl.pallas_call(
        kernel,
        out_shape=out_shape,
        in_specs=[smem] * len(scalars) + [vmem] * len(arrays),
        out_specs=jax.tree.map(lambda _: vmem, out_shape),
        scratch_shapes=[pltpu.VMEM(dims, BF) for dims in scratch],
        compiler_params=pltpu.CompilerParams(vmem_limit_bytes=limit * MB),
        cost_estimate=pl.CostEstimate(
            flops=flops, bytes_accessed=sum(a.size * 2 for a in arrays), transcendentals=0
        ),
    )(*scalars, *arrays)


def move(value, function):
    return lax.ppermute(value, "tensor", [(t, function(t)) for t in range(16)])


def send_four(values):
    masks = (1, 8, 9)
    got = {m: move(v, lambda t, m=m: t ^ m) for m, v in reversed(list(zip(masks, values)))}
    return [got[m] for m in masks]


def shift(value, quarters):
    return move(value, lambda t: t // 8 * 8 + (t + 2 * quarters) % 8)


def shards(hidden, out_grad, weight, first_moment, second_moment, next_hidden):
    block = first_moment.shape[0]
    tokens, units = hidden.shape
    features = out_grad.shape[1]
    cuts = (0, units // 3 * 2, units)
    sizes = [cuts[p + 1] - cuts[p] for p in range(PARTS)]
    index = lax.axis_index(("dp", "tensor")).reshape(1)
    product = tokens * units * features

    def parts(rows, dtype=BF):
        return tuple(shape(rows, size, dtype=dtype) for size in sizes)

    hidden_got = swap_cores(hidden)
    own, other = call(
        functools.partial(turn, block),
        (shape(features // 2, tokens), shape(features // 2, tokens)),
        [index],
        [out_grad],
        [(features, tokens)],
    )
    got = swap_cores(other)
    scratch = [(PARTS, 4 * block, 2 * tokens), (2 * tokens, units)]
    sent = call(
        functools.partial(grad_sent, cuts, block),
        parts(4 * block),
        [index],
        [own, got, hidden, hidden_got],
        scratch,
        flops=product,
    )
    arrived = [swap(sent[p], SCATTER, p, 0) for p in range(PARTS)]
    next_got = swap_cores(next_hidden)
    moments = shape(block, units, dtype=F32)
    input_grad, arranged, current, *kept = call(
        functools.partial(grad_kept, cuts, block),
        (shape(tokens, units), shape(2 * tokens, units), moments)
        + parts(4 * block),
        [index],
        [own, got, hidden, hidden_got, out_grad, weight, next_hidden, next_got],
        scratch + [(256, units)],
        flops=3 * product,
        limit=28,
    )

    def pairs(upper, lower):
        return [array for p in range(PARTS) for array in (upper[p], lower[p])]

    for step in (1, 2):
        rows = 4 * block >> step
        sums = call(
            functools.partial(add_parts, rows),
            parts(rows) + parts(rows, F32),
            [],
            pairs(kept, arrived),
        )
        arrived, kept = [swap(sums[p], SCATTER, p, step) for p in range(PARTS)], sums[PARTS:]
    inputs = [first_moment, second_moment, current] + pairs(kept, arrived)
    held = call(functools.partial(adam, cuts, False), parts(block), [], inputs)
    first_new, second_new, new_weight = call(
        functools.partial(adam, cuts, True), (moments, moments, shape(block, units)), [], inputs
    )

    for step in (2, 1, 0):
        arrived = [swap(held[p], GATHER, p, step) for p in range(PARTS)]
        if step:
            held = call(join_parts, parts(8 * block >> step), [], pairs(held, arrived))

    wide = features // 2
    rows = tokens // 2
    *sent, full = call(
        functools.partial(product_sent, cuts, block),
        (shape(rows, wide),) * 3 + (shape(wide, units),),
        [index],
        [arranged] + pairs(held, arrived),
        flops=product * 3 // 2,
    )
    arrived = send_four(sent)
    kept = call(
        product_kept, shape(rows, wide, dtype=F32), [], [arranged, full], flops=product // 2
    )
    quarters = call(
        add_quarters,
        (shape(32, wide, dtype=F32),) + (shape(32, wide),) * 3,
        [],
        [kept] + arrived,
    )
    share, lacking = call(
        add_shares,
        (shape(16, wide), shape(16, wide)),
        [],
        [quarters[0]] + [shift(quarters[k], k) for k in (2, 1, 3)],
    )
    value = call(
        functools.partial(weave, block),
        shape(16, features),
        [index],
        [share, swap_cores(lacking)],
    )

    others = {k: shift(value, k) for k in (2, 1, 3)}
    out = call(join_quarters, shape(64, features), [], [value] + [others[k] for k in (1, 2, 3)])
    next_out = call(place_rows, shape(tokens, features), [index], [out] + send_four([out] * 3))
    return (input_grad, first_new, second_new, new_weight, next_out)


def solution(mesh):
    placed = (
        P("dp", "tensor"),
        P("dp", None),
        P("tensor", None),
        P("dp", "tensor"),
        P("dp", "tensor"),
        P("dp", "tensor"),
    )
    return jax.shard_map(
        shards,
        mesh=mesh,
        in_specs=placed,
        out_specs=(
            P("dp", "tensor"),
            P("dp", "tensor"),
            P("dp", "tensor"),
            P("dp", "tensor"),
            P("dp", None),
        ),
        check_vma=False,
    )
```

```python
import functools

import jax
import jax.numpy as jnp
import numpy as np
from jax import lax
from jax.experimental import pallas as pl
from jax.experimental.pallas import tpu as pltpu
from jax.sharding import PartitionSpec as P

beta_first = 0.9
beta_second = 0.95
learn_rate = 0.001
weight_decay = 0.1
epsilon = 1e-08
correct_first = 0.999973438601112
correct_second = 0.99407947077967

BF = jnp.bfloat16
F32 = jnp.float32
MB = 1024 * 1024

GRAY = (0, 1, 3, 2)
CORE, X1, X2, Y = 1, 2, 4, 8
ENC = [(d % 2) | (GRAY[(d // 2) % 4] << 1) | ((d // 8) << 3) for d in range(16)]
DEC = [ENC.index(r) for r in range(16)]
SCATTER = (((X1, X2, Y), (X2, Y, X1)), ((Y, X1, X2), (Y, X1, X2)))
GATHER = (((X2, Y, X1), (X1, X2, Y)), ((Y, X1, X2), (Y, X1, X2)))
PARTS = 2


def flip(masks):
    return [(d, DEC[ENC[d] ^ masks[d % 2]]) for d in range(16)]


def relative(order, q):
    return (q >> 2 & 1) * order[0] | (q >> 1 & 1) * order[1] | (q & 1) * order[2]


def swap(value, orders, part, step):
    return lax.ppermute(value, "dp", flip([order[step] for order in orders[part]]))


def swap_cores(value):
    return lax.ppermute(value, "dp", flip((CORE, CORE)))


def aligned(index, size):
    return pl.ds(pl.multiple_of(index * size, size), size)


def place(device, orders, part, q):
    first, second = orders[part]
    move = jnp.where(device % 2 == 0, relative(first, q), relative(second, q)) // 2
    x = device // 2 % 4
    moved = ((x ^ (x // 2)) + device // 8 * 4) ^ move
    gray = moved % 4
    return moved - gray + (gray ^ (gray // 2))


def turn(block, index, out_grad, own, other, turned):
    turned[...] = out_grad[...].T
    parity = index[0] // 16 % 2
    for i in range(8):
        rows = slice(i * block, (i + 1) * block)
        own[rows, :] = turned[aligned(2 * i + parity, block), :]
        other[rows, :] = turned[aligned(2 * i + 1 - parity, block), :]


def grad_half(start, cuts, block, index, own, got, hidden, hidden_got, outs, lhs, rhs):
    tokens = hidden.shape[0]
    rhs[:tokens, :] = hidden[...]
    rhs[tokens:, :] = hidden_got[...]
    for part in range(PARTS):
        for q in range(4):
            rows = slice(q * block, (q + 1) * block)
            from_rows = aligned(place(index[0] // 16, SCATTER, part, start + q), block)
            lhs[part, rows, :tokens] = own[from_rows, :]
            lhs[part, rows, tokens:] = got[from_rows, :]
        outs[part][...] = jnp.dot(
            lhs[part], rhs[:, cuts[part] : cuts[part + 1]], preferred_element_type=F32
        ).astype(BF)


def grad_sent(cuts, block, index, own, got, hidden, hidden_got, *rest):
    grad_half(4, cuts, block, index, own, got, hidden, hidden_got, rest[:PARTS], *rest[PARTS:])


def grad_kept(
    cuts, block, index, own, got, hidden, hidden_got, out_grad, weight, nexts, nexts_got, *rest
):
    input_grad, arranged, current = rest[:3]
    rest, turned = rest[3:-1], rest[-1]
    grad_half(0, cuts, block, index, own, got, hidden, hidden_got, rest[:PARTS], *rest[PARTS:])
    input_grad[...] = contract(out_grad, weight)
    first = index[0] // 16 * block
    columns = pl.ds(pl.multiple_of(first // 128 * 128, 128), turned.shape[0])
    turned[...] = weight[:, columns].T
    current[...] = turned[pl.ds(pl.multiple_of(first % 128, 16), block), :].astype(F32)
    for at, owner in enumerate(owners(index[0] % 16, 1)):
        rows = aligned(owner, 16)
        arranged[32 * at : 32 * at + 16, :] = nexts[rows, :]
        arranged[32 * at + 16 : 32 * at + 32, :] = nexts_got[rows, :]


def owners(tensor, sign):
    upper, low, quarter = tensor // 8, tensor % 2, tensor % 8 // 2
    for y in range(2):
        for b in range(2):
            for k in range(4):
                yield (upper + y) % 2 * 8 + (quarter + sign * k + 4) % 4 * 2 + (low + b) % 2


def total(terms, rows):
    result = terms[0][rows, :].astype(F32)
    for term in terms[1:]:
        result = result + term[rows, :].astype(F32)
    return result


def add_parts(size, *refs):
    terms, outs = refs[: -2 * PARTS], refs[-2 * PARTS :]
    for part in range(PARTS):
        mine = terms[2 * part : 2 * part + 2]
        outs[part][...] = total(mine, slice(size, 2 * size)).astype(BF)
        outs[PARTS + part][...] = total(mine, slice(0, size))


def join_parts(*refs):
    for part in range(PARTS):
        upper, lower = refs[2 * part : 2 * part + 2]
        out = refs[2 * PARTS + part]
        rows = upper.shape[0]
        out[:rows, :] = upper[...]
        out[rows:, :] = lower[...]


def adam(cuts, stored, first_moment, second_moment, current, *refs):
    terms, outs = refs[: 2 * PARTS], refs[2 * PARTS :]
    for part in range(PARTS):
        columns = slice(cuts[part], cuts[part + 1])
        grad = total(terms[2 * part : 2 * part + 2], slice(None))
        first_new = beta_first * first_moment[:, columns] + (1.0 - beta_first) * grad
        second_new = beta_second * second_moment[:, columns] + (1.0 - beta_second) * grad * grad
        update = first_new / correct_first / (jnp.sqrt(second_new / correct_second) + epsilon)
        old = current[:, columns]
        new_weight = (old - learn_rate * (update + weight_decay * old)).astype(BF)
        if stored:
            outs[0][:, columns] = first_new
            outs[1][:, columns] = second_new
            outs[2][:, columns] = new_weight
        else:
            outs[part][...] = new_weight


def contract(one, two):
    return lax.dot_general(
        one[...], two[...], (((1,), (1,)), ((), ())), preferred_element_type=F32
    ).astype(BF)


def product_sent(cuts, block, index, arranged, *rest):
    pieces, outs, full = rest[: 2 * PARTS], rest[2 * PARTS : -1], rest[-1]
    for part in range(PARTS):
        columns = slice(cuts[part], cuts[part + 1])
        for q in range(8):
            ref = pieces[2 * part + q // 4]
            to_rows = aligned(place(index[0] // 16, GATHER, part, q), block)
            full[to_rows, columns] = ref[q % 4 * block : (q % 4 + 1) * block, :]
    rows = outs[0].shape[0]
    value = contract(arranged.at[rows:], full)
    for k, out in enumerate(outs):
        out[...] = value[k * rows : (k + 1) * rows]


def product_kept(arranged, full, out):
    out[...] = lax.dot_general(
        arranged[: out.shape[0], :],
        full[...],
        (((1,), (1,)), ((), ())),
        preferred_element_type=F32,
    )


def add_quarters(*refs):
    terms, outs = refs[:4], refs[4:]
    for k in range(4):
        outs[k][...] = total(terms, slice(32 * k, 32 * k + 32)).astype(outs[k].dtype)


def add_shares(one, two, three, four, own, other):
    value = total((one, two, three, four), slice(None))
    own[...] = value[:16].astype(BF)
    other[...] = value[16:].astype(BF)


def weave(block, index, own, got, out):
    parity = index[0] // 16 % 2
    mine, theirs = own[...].astype(F32), got[...].astype(F32)
    even = jnp.where(parity == 0, mine, theirs)
    odd = jnp.where(parity == 0, theirs, mine)
    pieces = []
    for i in range(8):
        columns = slice(i * block, (i + 1) * block)
        pieces += [even[:, columns], odd[:, columns]]
    out[...] = jnp.concatenate(pieces, axis=1).astype(BF)


def join_quarters(own, one, three, two, out):
    for k, ref in enumerate((own, one, two, three)):
        out[16 * k : 16 * k + 16, :] = ref[...]


def place_rows(index, own, both, upper, low, out):
    quarters = (own, low, upper, both)
    for at, owner in enumerate(owners(index[0] % 16, -1)):
        rows = at % 4 * 16
        out[aligned(owner, 16), :] = quarters[at // 4][rows : rows + 16, :]


def shape(*dims, dtype=BF):
    return jax.ShapeDtypeStruct(dims, dtype)


def call(kernel, out_shape, scalars, arrays, scratch=(), flops=0, limit=16):
    vmem = pl.BlockSpec(memory_space=pltpu.VMEM)
    smem = pl.BlockSpec(memory_space=pltpu.SMEM)
    return pl.pallas_call(
        kernel,
        out_shape=out_shape,
        in_specs=[smem] * len(scalars) + [vmem] * len(arrays),
        out_specs=jax.tree.map(lambda _: vmem, out_shape),
        scratch_shapes=[pltpu.VMEM(dims, BF) for dims in scratch],
        compiler_params=pltpu.CompilerParams(vmem_limit_bytes=limit * MB),
        cost_estimate=pl.CostEstimate(
            flops=flops, bytes_accessed=sum(a.size * 2 for a in arrays), transcendentals=0
        ),
    )(*scalars, *arrays)


def move(value, function):
    return lax.ppermute(value, "tensor", [(t, function(t)) for t in range(16)])


def send_four(values):
    masks = (1, 8, 9)
    got = {m: move(v, lambda t, m=m: t ^ m) for m, v in reversed(list(zip(masks, values)))}
    return [got[m] for m in masks]


def shift(value, quarters):
    return move(value, lambda t: t // 8 * 8 + (t + 2 * quarters) % 8)


def shards(hidden, out_grad, weight, first_moment, second_moment, next_hidden):
    block = first_moment.shape[0]
    tokens, units = hidden.shape
    features = out_grad.shape[1]
    cuts = (0, units // 3 * 2, units)
    sizes = [cuts[p + 1] - cuts[p] for p in range(PARTS)]
    index = lax.axis_index(("dp", "tensor")).reshape(1)
    product = tokens * units * features

    def parts(rows, dtype=BF):
        return tuple(shape(rows, size, dtype=dtype) for size in sizes)

    hidden_got = swap_cores(hidden)
    own, other = call(
        functools.partial(turn, block),
        (shape(features // 2, tokens), shape(features // 2, tokens)),
        [index],
        [out_grad],
        [(features, tokens)],
    )
    got = swap_cores(other)
    scratch = [(PARTS, 4 * block, 2 * tokens), (2 * tokens, units)]
    sent = call(
        functools.partial(grad_sent, cuts, block),
        parts(4 * block),
        [index],
        [own, got, hidden, hidden_got],
        scratch,
        flops=product,
    )
    arrived = [swap(sent[p], SCATTER, p, 0) for p in range(PARTS)]
    next_got = swap_cores(next_hidden)
    moments = shape(block, units, dtype=F32)
    input_grad, arranged, current, *kept = call(
        functools.partial(grad_kept, cuts, block),
        (shape(tokens, units), shape(2 * tokens, units), moments)
        + parts(4 * block),
        [index],
        [own, got, hidden, hidden_got, out_grad, weight, next_hidden, next_got],
        scratch + [(256, units)],
        flops=3 * product,
        limit=28,
    )

    def pairs(upper, lower):
        return [array for p in range(PARTS) for array in (upper[p], lower[p])]

    for step in (1, 2):
        rows = 4 * block >> step
        sums = call(
            functools.partial(add_parts, rows),
            parts(rows) + parts(rows, F32),
            [],
            pairs(kept, arrived),
        )
        arrived, kept = [swap(sums[p], SCATTER, p, step) for p in range(PARTS)], sums[PARTS:]
    inputs = [first_moment, second_moment, current] + pairs(kept, arrived)
    held = call(functools.partial(adam, cuts, False), parts(block), [], inputs)
    first_new, second_new, new_weight = call(
        functools.partial(adam, cuts, True), (moments, moments, shape(block, units)), [], inputs
    )

    for step in (2, 1, 0):
        arrived = [swap(held[p], GATHER, p, step) for p in range(PARTS)]
        if step:
            held = call(join_parts, parts(8 * block >> step), [], pairs(held, arrived))

    wide = features // 2
    rows = tokens // 2
    *sent, full = call(
        functools.partial(product_sent, cuts, block),
        (shape(rows, wide),) * 3 + (shape(wide, units),),
        [index],
        [arranged] + pairs(held, arrived),
        flops=product * 3 // 2,
    )
    arrived = send_four(sent)
    kept = call(
        product_kept, shape(rows, wide, dtype=F32), [], [arranged, full], flops=product // 2
    )
    quarters = call(
        add_quarters,
        (shape(32, wide, dtype=F32),) + (shape(32, wide),) * 3,
        [],
        [kept] + arrived,
    )
    share, lacking = call(
        add_shares,
        (shape(16, wide), shape(16, wide)),
        [],
        [quarters[0]] + [shift(quarters[k], k) for k in (2, 1, 3)],
    )
    value = call(
        functools.partial(weave, block),
        shape(16, features),
        [index],
        [share, swap_cores(lacking)],
    )

    others = [shift(value, k) for k in (1, 3, 2)]
    out = call(join_quarters, shape(64, features), [], [value] + others)
    next_out = call(
        place_rows, shape(tokens, features), [index], [out] + send_four([out] * 3)[::-1]
    )
    return (input_grad, first_new, second_new, new_weight, next_out)


def solution(mesh):
    placed = (
        P("dp", "tensor"),
        P("dp", None),
        P("tensor", None),
        P("dp", "tensor"),
        P("dp", "tensor"),
        P("dp", "tensor"),
    )
    return jax.shard_map(
        shards,
        mesh=mesh,
        in_specs=placed,
        out_specs=(
            P("dp", "tensor"),
            P("dp", "tensor"),
            P("dp", "tensor"),
            P("dp", "tensor"),
            P("dp", None),
        ),
        check_vma=False,
    )
```

```python
import functools

import jax
import jax.numpy as jnp
import numpy as np
from jax import lax
from jax.experimental import pallas as pl
from jax.experimental.pallas import tpu as pltpu
from jax.sharding import PartitionSpec as P

beta_first = 0.9
beta_second = 0.95
learn_rate = 0.001
weight_decay = 0.1
epsilon = 1e-08
correct_first = 0.999973438601112
correct_second = 0.99407947077967

BF = jnp.bfloat16
F32 = jnp.float32
MB = 1024 * 1024

GRAY = (0, 1, 3, 2)
CORE, X1, X2, Y = 1, 2, 4, 8
ENC = [(d % 2) | (GRAY[(d // 2) % 4] << 1) | ((d // 8) << 3) for d in range(16)]
DEC = [ENC.index(r) for r in range(16)]
SCATTER = (((X2, Y, X1), (X1, X2, Y)), ((Y, X1, X2), (Y, X1, X2)))
GATHER = (((X2, Y, X1), (X1, X2, Y)), ((Y, X1, X2), (Y, X1, X2)))
PARTS = 2


def flip(masks):
    return [(d, DEC[ENC[d] ^ masks[d % 2]]) for d in range(16)]


def relative(order, q):
    return (q >> 2 & 1) * order[0] | (q >> 1 & 1) * order[1] | (q & 1) * order[2]


def swap(value, orders, part, step):
    return lax.ppermute(value, "dp", flip([order[step] for order in orders[part]]))


def swap_cores(value):
    return lax.ppermute(value, "dp", flip((CORE, CORE)))


def aligned(index, size):
    return pl.ds(pl.multiple_of(index * size, size), size)


def place(device, orders, part, q):
    first, second = orders[part]
    move = jnp.where(device % 2 == 0, relative(first, q), relative(second, q)) // 2
    x = device // 2 % 4
    moved = ((x ^ (x // 2)) + device // 8 * 4) ^ move
    gray = moved % 4
    return moved - gray + (gray ^ (gray // 2))


def turn(block, index, out_grad, own, other, turned):
    turned[...] = out_grad[...].T
    parity = index[0] // 16 % 2
    for i in range(8):
        rows = slice(i * block, (i + 1) * block)
        own[rows, :] = turned[aligned(2 * i + parity, block), :]
        other[rows, :] = turned[aligned(2 * i + 1 - parity, block), :]


def grad_half(start, cuts, block, index, own, got, hidden, hidden_got, outs, lhs, rhs):
    tokens = hidden.shape[0]
    rhs[:tokens, :] = hidden[...]
    rhs[tokens:, :] = hidden_got[...]
    for part in range(PARTS):
        for q in range(4):
            rows = slice(q * block, (q + 1) * block)
            from_rows = aligned(place(index[0] // 16, SCATTER, part, start + q), block)
            lhs[part, rows, :tokens] = own[from_rows, :]
            lhs[part, rows, tokens:] = got[from_rows, :]
        outs[part][...] = jnp.dot(
            lhs[part], rhs[:, cuts[part] : cuts[part + 1]], preferred_element_type=F32
        ).astype(BF)


def grad_sent(cuts, block, index, own, got, hidden, hidden_got, *rest):
    grad_half(4, cuts, block, index, own, got, hidden, hidden_got, rest[:PARTS], *rest[PARTS:])


def grad_kept(
    cuts, block, index, own, got, hidden, hidden_got, out_grad, weight, nexts, nexts_got, *rest
):
    input_grad, arranged, current = rest[:3]
    rest, turned = rest[3:-1], rest[-1]
    grad_half(0, cuts, block, index, own, got, hidden, hidden_got, rest[:PARTS], *rest[PARTS:])
    input_grad[...] = contract(out_grad, weight)
    first = index[0] // 16 * block
    columns = pl.ds(pl.multiple_of(first // 128 * 128, 128), turned.shape[0])
    turned[...] = weight[:, columns].T
    current[...] = turned[pl.ds(pl.multiple_of(first % 128, 16), block), :].astype(F32)
    for at, owner in enumerate(owners(index[0] % 16, 1)):
        rows = aligned(owner, 16)
        arranged[32 * at : 32 * at + 16, :] = nexts[rows, :]
        arranged[32 * at + 16 : 32 * at + 32, :] = nexts_got[rows, :]


def owners(tensor, sign):
    upper, low, quarter = tensor // 8, tensor % 2, tensor % 8 // 2
    for y in range(2):
        for b in range(2):
            for k in range(4):
                yield (upper + y) % 2 * 8 + (quarter + sign * k + 4) % 4 * 2 + (low + b) % 2


def total(terms, rows):
    result = terms[0][rows, :].astype(F32)
    for term in terms[1:]:
        result = result + term[rows, :].astype(F32)
    return result


def add_parts(size, *refs):
    terms, outs = refs[: -2 * PARTS], refs[-2 * PARTS :]
    for part in range(PARTS):
        mine = terms[2 * part : 2 * part + 2]
        outs[part][...] = total(mine, slice(size, 2 * size)).astype(BF)
        outs[PARTS + part][...] = total(mine, slice(0, size))


def join_parts(*refs):
    for part in range(PARTS):
        upper, lower = refs[2 * part : 2 * part + 2]
        out = refs[2 * PARTS + part]
        rows = upper.shape[0]
        out[:rows, :] = upper[...]
        out[rows:, :] = lower[...]


def adam(cuts, stored, first_moment, second_moment, current, *refs):
    terms, outs = refs[: 2 * PARTS], refs[2 * PARTS :]
    for part in range(PARTS):
        columns = slice(cuts[part], cuts[part + 1])
        grad = total(terms[2 * part : 2 * part + 2], slice(None))
        first_new = beta_first * first_moment[:, columns] + (1.0 - beta_first) * grad
        second_new = beta_second * second_moment[:, columns] + (1.0 - beta_second) * grad * grad
        update = first_new / correct_first / (jnp.sqrt(second_new / correct_second) + epsilon)
        old = current[:, columns]
        new_weight = (old - learn_rate * (update + weight_decay * old)).astype(BF)
        if stored:
            outs[0][:, columns] = first_new
            outs[1][:, columns] = second_new
            outs[2][:, columns] = new_weight
        else:
            outs[part][...] = new_weight


def contract(one, two):
    return lax.dot_general(
        one[...], two[...], (((1,), (1,)), ((), ())), preferred_element_type=F32
    ).astype(BF)


def product_sent(cuts, block, index, arranged, *rest):
    pieces, outs, full = rest[: 2 * PARTS], rest[2 * PARTS : -1], rest[-1]
    for part in range(PARTS):
        columns = slice(cuts[part], cuts[part + 1])
        for q in range(8):
            ref = pieces[2 * part + q // 4]
            to_rows = aligned(place(index[0] // 16, GATHER, part, q), block)
            full[to_rows, columns] = ref[q % 4 * block : (q % 4 + 1) * block, :]
    rows = outs[0].shape[0]
    value = contract(arranged.at[rows:], full)
    for k, out in enumerate(outs):
        out[...] = value[k * rows : (k + 1) * rows]


def product_kept(arranged, full, out):
    out[...] = lax.dot_general(
        arranged[: out.shape[0], :],
        full[...],
        (((1,), (1,)), ((), ())),
        preferred_element_type=F32,
    )


def add_quarters(*refs):
    terms, outs = refs[:4], refs[4:]
    for k in range(4):
        outs[k][...] = total(terms, slice(32 * k, 32 * k + 32)).astype(outs[k].dtype)


def add_shares(one, two, three, four, own, other):
    value = total((one, two, three, four), slice(None))
    own[...] = value[:16].astype(BF)
    other[...] = value[16:].astype(BF)


def weave(block, index, own, got, out):
    parity = index[0] // 16 % 2
    mine, theirs = own[...].astype(F32), got[...].astype(F32)
    even = jnp.where(parity == 0, mine, theirs)
    odd = jnp.where(parity == 0, theirs, mine)
    pieces = []
    for i in range(8):
        columns = slice(i * block, (i + 1) * block)
        pieces += [even[:, columns], odd[:, columns]]
    out[...] = jnp.concatenate(pieces, axis=1).astype(BF)


def join_quarters(own, one, three, two, out):
    for k, ref in enumerate((own, one, two, three)):
        out[16 * k : 16 * k + 16, :] = ref[...]


def place_rows(index, own, both, upper, low, out):
    quarters = (own, low, upper, both)
    for at, owner in enumerate(owners(index[0] % 16, -1)):
        rows = at % 4 * 16
        out[aligned(owner, 16), :] = quarters[at // 4][rows : rows + 16, :]


def shape(*dims, dtype=BF):
    return jax.ShapeDtypeStruct(dims, dtype)


def call(kernel, out_shape, scalars, arrays, scratch=(), flops=0, limit=16):
    vmem = pl.BlockSpec(memory_space=pltpu.VMEM)
    smem = pl.BlockSpec(memory_space=pltpu.SMEM)
    return pl.pallas_call(
        kernel,
        out_shape=out_shape,
        in_specs=[smem] * len(scalars) + [vmem] * len(arrays),
        out_specs=jax.tree.map(lambda _: vmem, out_shape),
        scratch_shapes=[pltpu.VMEM(dims, BF) for dims in scratch],
        compiler_params=pltpu.CompilerParams(vmem_limit_bytes=limit * MB),
        cost_estimate=pl.CostEstimate(
            flops=flops, bytes_accessed=sum(a.size * 2 for a in arrays), transcendentals=0
        ),
    )(*scalars, *arrays)


def move(value, function):
    return lax.ppermute(value, "tensor", [(t, function(t)) for t in range(16)])


def send_four(values):
    masks = (1, 8, 9)
    got = {m: move(v, lambda t, m=m: t ^ m) for m, v in reversed(list(zip(masks, values)))}
    return [got[m] for m in masks]


def shift(value, quarters):
    return move(value, lambda t: t // 8 * 8 + (t + 2 * quarters) % 8)


def shards(hidden, out_grad, weight, first_moment, second_moment, next_hidden):
    block = first_moment.shape[0]
    tokens, units = hidden.shape
    features = out_grad.shape[1]
    cuts = (0, units // 3 * 2, units)
    sizes = [cuts[p + 1] - cuts[p] for p in range(PARTS)]
    index = lax.axis_index(("dp", "tensor")).reshape(1)
    product = tokens * units * features

    def parts(rows, dtype=BF):
        return tuple(shape(rows, size, dtype=dtype) for size in sizes)

    hidden_got = swap_cores(hidden)
    own, other = call(
        functools.partial(turn, block),
        (shape(features // 2, tokens), shape(features // 2, tokens)),
        [index],
        [out_grad],
        [(features, tokens)],
    )
    got = swap_cores(other)
    scratch = [(PARTS, 4 * block, 2 * tokens), (2 * tokens, units)]
    sent = call(
        functools.partial(grad_sent, cuts, block),
        parts(4 * block),
        [index],
        [own, got, hidden, hidden_got],
        scratch,
        flops=product,
    )
    arrived = [swap(sent[p], SCATTER, p, 0) for p in range(PARTS)]
    next_got = swap_cores(next_hidden)
    moments = shape(block, units, dtype=F32)
    input_grad, arranged, current, *kept = call(
        functools.partial(grad_kept, cuts, block),
        (shape(tokens, units), shape(2 * tokens, units), moments)
        + parts(4 * block),
        [index],
        [own, got, hidden, hidden_got, out_grad, weight, next_hidden, next_got],
        scratch + [(256, units)],
        flops=3 * product,
        limit=28,
    )

    def pairs(upper, lower):
        return [array for p in range(PARTS) for array in (upper[p], lower[p])]

    for step in (1, 2):
        rows = 4 * block >> step
        sums = call(
            functools.partial(add_parts, rows),
            parts(rows) + parts(rows, F32),
            [],
            pairs(kept, arrived),
        )
        arrived, kept = [swap(sums[p], SCATTER, p, step) for p in range(PARTS)], sums[PARTS:]
    inputs = [first_moment, second_moment, current] + pairs(kept, arrived)
    held = call(functools.partial(adam, cuts, False), parts(block), [], inputs)
    first_new, second_new, new_weight = call(
        functools.partial(adam, cuts, True), (moments, moments, shape(block, units)), [], inputs
    )

    for step in (2, 1, 0):
        arrived = [swap(held[p], GATHER, p, step) for p in range(PARTS)]
        if step:
            held = call(join_parts, parts(8 * block >> step), [], pairs(held, arrived))

    wide = features // 2
    rows = tokens // 2
    *sent, full = call(
        functools.partial(product_sent, cuts, block),
        (shape(rows, wide),) * 3 + (shape(wide, units),),
        [index],
        [arranged] + pairs(held, arrived),
        flops=product * 3 // 2,
    )
    arrived = send_four(sent)
    kept = call(
        product_kept, shape(rows, wide, dtype=F32), [], [arranged, full], flops=product // 2
    )
    quarters = call(
        add_quarters,
        (shape(32, wide, dtype=F32),) + (shape(32, wide),) * 3,
        [],
        [kept] + arrived,
    )
    share, lacking = call(
        add_shares,
        (shape(16, wide), shape(16, wide)),
        [],
        [quarters[0]] + [shift(quarters[k], k) for k in (2, 1, 3)],
    )
    value = call(
        functools.partial(weave, block),
        shape(16, features),
        [index],
        [share, swap_cores(lacking)],
    )

    others = [shift(value, k) for k in (1, 3, 2)]
    out = call(join_quarters, shape(64, features), [], [value] + others)
    next_out = call(
        place_rows, shape(tokens, features), [index], [out] + send_four([out] * 3)[::-1]
    )
    return (input_grad, first_new, second_new, new_weight, next_out)


def solution(mesh):
    placed = (
        P("dp", "tensor"),
        P("dp", None),
        P("tensor", None),
        P("dp", "tensor"),
        P("dp", "tensor"),
        P("dp", "tensor"),
    )
    return jax.shard_map(
        shards,
        mesh=mesh,
        in_specs=placed,
        out_specs=(
            P("dp", "tensor"),
            P("dp", "tensor"),
            P("dp", "tensor"),
            P("dp", "tensor"),
            P("dp", None),
        ),
        check_vma=False,
    )
```
